512 devices in a mesh: depth: 32 (over z, x), tile: 16 (over y, core).
Axes of the slice: x: 4, y: 8, z: 8, core: 2. Of those that a mesh axis runs over, the one named last changes fastest.
Arguments:
- density: bfloat16 [1024, 128, 2048], P('depth', None, 'tile'), may hold values from 0.25 to 4
- heat: bfloat16 [1024, 128, 2048], P('depth', None, 'tile'), may hold values from 0.05 to 1
- emit_color: float32 [3], replicated, may hold values from 0.2 to 1.5
- albedo: float32 [3], replicated, may hold values from 0.2 to 1.2
- hot_order: int32 [16, 16], P('tile'), may hold values from 0 to 15, each once within a row
- hot_count: int32 [16], P('tile'), may hold values from 1 to 4, 40 in all
Outputs:
- image: float32 [4, 16, 16384], P(None, 'tile', 'depth')
The draws below stay inside these ranges and needn't reach their ends.
Inputs may be any that keep to these rules, and one draw needn't show every extreme that they name: `hot_order`: each row lists each of the 16 bricks of its tile group once.
All inputs are finite; a program needn't handle non-finite values. No bound on the sum of `hot_count` on one device may be relied on, other than what follows from the above.
Results may differ from the reference program's by a relative error of at most 0.0033.
Values may be sent and summed in bfloat16 or wider, within the bound.
A program may use at most 64 MiB of HBM per device.

```python
import math
import jax
import jax.numpy as jnp
import numpy as np
from jax import lax

TW = 128
BW = 32
HOT = 4
NZ = 1024
SCREEN_W = 2048
BPT = 16
HOTALL = 64
N_TILE = 16


def draw_heat(key, part):
    key = jax.random.fold_in(key, 7)
    column_key, voxel_key = jax.random.split(key)
    column = jnp.exp(jax.random.uniform(column_key, (1, TW, SCREEN_W), jnp.float32, math.log(0.2), 0.0))
    voxel = jax.random.uniform(voxel_key, (NZ, TW, SCREEN_W), jnp.float32, 0.25, 1.0)
    return (column * voxel).astype(jnp.bfloat16)


def block_levels(own_key, shape, shards, low, largest):
    loudness = 1.0
    for position, parts in shards:
        steps = jax.random.uniform(jax.random.fold_in(jax.random.fold_in(own_key, 6), position), (parts,), jnp.float32, low / len(shards), largest / len(shards))
        loudness = loudness * jnp.repeat(jnp.exp(steps), shape[position] // parts).reshape((-1,) + (1,) * (len(shape) - 1 - position))
    return loudness


def length_profile(count, total, bound, lean):
    weights = [(1 << 20) // math.isqrt(standing ** lean) + 1 for standing in range(2, count + 1)]
    surplus, counts = total - bound - (count - 1), [1] * (count - 1)
    while surplus > 0:
        free = [i for i in range(count - 1) if counts[i] < bound]
        pool, remaining = sum([weights[i] for i in free]), surplus
        for i in free:
            addition = min(bound - counts[i], max(1, remaining * weights[i] // pool), surplus)
            counts[i] = counts[i] + addition
            surplus = surplus - addition
    return np.array([bound] + counts)


def ragged(stream_key, number_of, total, reach, skew):
    if number_of == 2:
        one = jax.random.randint(stream_key, (), max(1, total - reach), min(reach, total - 1) + 1)
        return jnp.stack([one, total - one])
    sizes = jnp.asarray(length_profile(number_of, total, reach, skew), jnp.int32)
    pairs = (number_of - 1) // 2
    donor, taker = sizes[1:1 + 2 * pairs:2], sizes[2:2 + 2 * pairs:2]
    margin = jnp.minimum(donor - 1, reach - taker)
    moved = jax.random.randint(jax.random.fold_in(stream_key, 1), (pairs,), 0, 1 << 20) % (margin + 1)
    sizes = sizes.at[1:1 + 2 * pairs:2].set(donor - moved).at[2:2 + 2 * pairs:2].set(taker + moved)
    return sizes[jax.random.permutation(jax.random.fold_in(stream_key, 2), number_of)]


def setup_inputs(seed: int = 0) -> dict:
    arg_keys = jax.random.split(jax.random.key(seed), 7)
    return {
        "density": jnp.clip(jnp.exp(math.log(4.0) - 2.7725887 * jax.random.uniform(arg_keys[0], (NZ, TW, SCREEN_W), jnp.float32) ** block_levels(arg_keys[0], (NZ, TW, SCREEN_W), ((0, 32), (2, 16)), -0.2, 0.2)), 0.25, 4.0).astype(jnp.bfloat16),
        "heat": draw_heat(jax.random.fold_in(arg_keys[6], 71), 0),
        "emit_color": jnp.clip(jax.random.uniform(arg_keys[2], (3,), jnp.float32, 0.2, 1.5), 0.2, 1.5),
        "albedo": jnp.clip(jax.random.uniform(arg_keys[3], (3,), jnp.float32, 0.2, 1.2), 0.2, 1.2),
        "hot_order": jax.vmap(lambda own: jax.random.permutation(own, BPT))(jax.random.split(arg_keys[4], N_TILE)).reshape((N_TILE, BPT)).astype(jnp.int32),
        "hot_count": ragged(arg_keys[5], N_TILE, N_TILE * HOT // 2 + N_TILE // 2, HOT, 1).astype(jnp.int32),
    }


def glow(offsets, radius):
    turn = (offsets * offsets) % (2 * BW)
    phase = turn.astype(jnp.float32) * (math.pi / BW) + math.pi / 8.0
    ratio = offsets.astype(jnp.float32) / radius
    return jnp.cos(phase) / (1.0 + ratio * ratio)


def reference(density, heat, emit_color, albedo, hot_order, hot_count):
    optical = density.astype(jnp.float32) * (1.5 / NZ)
    behind = jnp.cumsum(optical[::-1], axis=0)[::-1] - optical
    lighting = jnp.exp(-behind)
    across = TW // BW
    chosen = hot_order[:, :HOT].astype(jnp.int32)
    live_slot = (jnp.arange(HOT, dtype=jnp.int32)[None, :] < hot_count[:, None]).astype(jnp.float32)
    anchor_x = (jnp.arange(N_TILE, dtype=jnp.int32)[:, None] * TW + (chosen % across) * BW).reshape(-1).astype(jnp.int32)
    anchor_y = ((chosen // across) * BW).reshape(-1).astype(jnp.int32)
    live_flat = live_slot.reshape(-1)

    def cut_brick(corner_y, corner_x):
        return lax.dynamic_slice(heat, (jnp.int32(0), corner_y, corner_x), (NZ, BW, BW))

    bricks = jax.vmap(cut_brick)(anchor_y, anchor_x).astype(jnp.float32)
    scale = 64.0 / (HOTALL * BW)
    inner = jnp.arange(BW, dtype=jnp.int32)
    pixels = jnp.arange(TW, dtype=jnp.int32)
    offsets_y = pixels[:, None, None] - (anchor_y[None, :, None] + inner[None, None, :])
    table_y = lax.optimization_barrier(glow(offsets_y, TW / 4.0).astype(jnp.bfloat16)).astype(jnp.float32)

    def per_tile(tile_index):
        screen_x = tile_index * TW + pixels
        offsets_x = screen_x[None, None, :] - (anchor_x[:, None, None] + inner[None, :, None])
        table_x = scale * live_flat[:, None, None] * glow(offsets_x, SCREEN_W / 2.0)
        table_x = lax.optimization_barrier(table_x.astype(jnp.bfloat16)).astype(jnp.float32)
        spread = jnp.einsum("hzvx,hxX->zhvX", bricks, table_x, precision=lax.Precision.HIGHEST)
        spread = lax.optimization_barrier(spread.astype(jnp.bfloat16)).astype(jnp.float32)
        return jnp.einsum("Yhv,zhvX->zYX", table_y, spread, precision=lax.Precision.HIGHEST)

    scattered = lax.map(per_tile, jnp.arange(N_TILE, dtype=jnp.int32))
    inscatter = jnp.transpose(scattered, (1, 2, 0, 3)).reshape(NZ, TW, SCREEN_W)
    heat_value = heat.astype(jnp.float32)
    opacity = 1.0 - jnp.exp(-optical)
    ahead = jnp.cumsum(optical, axis=0) - optical
    weight = opacity * jnp.exp(-ahead)
    lit = lighting + inscatter
    planes = []
    for channel in range(3):
        planes.append(jnp.sum(weight * (emit_color[channel] * heat_value + albedo[channel] * lit), axis=0))
    planes.append(1.0 - jnp.exp(-jnp.sum(optical, axis=0)))
    stacked = jnp.stack(planes)
    return stacked.reshape(4, TW, N_TILE, TW).transpose(0, 2, 1, 3).reshape(4, N_TILE, TW * TW)
```

```python
import functools
import math

import jax
import jax.numpy as jnp
from jax import lax
from jax.experimental import pallas as pl
from jax.experimental.pallas import tpu as pltpu
from jax.sharding import PartitionSpec as P

BW = 32
HOT = 4
QUARTERS = 4
F32 = jnp.float32
BF16 = jnp.bfloat16
MESH = pl.DeviceIdType.MESH


def iota(shape, axis):
    return lax.broadcasted_iota(jnp.int32, shape, axis)


def render(
    depth_count, tile_count,
    density_hbm, heat_hbm, emit, albedo, order, count,
    out_ref,
    density, heat, weight, blocks, spread, tables, cosines, table_y, meta, plane,
    early_out, early_in, late_out, late_in, before, base,
    copy_sem, own_send, own_recv, right_send, right_recv, left_send, left_recv,
    pair_right_send, pair_right_recv, pair_left_send, pair_left_recv,
    meta_send, meta_recv, early_send, early_recv, late_send, late_recv,
):
    slices, height, breadth = density.shape
    chips = tile_count // 2
    slots = chips - 1
    steps = 2 * slots
    zq = slices // QUARTERS
    rows = zq * BW
    band = height // depth_count
    depth = lax.axis_index("depth")
    tile = lax.axis_index("tile")
    chip = tile // 2
    core = tile % 2
    sibling = 2 * chip + 1 - core

    def at_tile(index):
        return (depth, index)

    def remote(src, dst, send, recv, device):
        return pltpu.make_async_remote_copy(
            src_ref=src, dst_ref=dst, send_sem=send, recv_sem=recv, device_id=device, device_id_type=MESH
        )

    heat_copy = pltpu.make_async_copy(heat_hbm, heat, copy_sem.at[0])
    density_copy = pltpu.make_async_copy(density_hbm, density, copy_sem.at[1])
    heat_copy.start()
    density_copy.start()

    barrier = pltpu.get_barrier_semaphore()

    @pl.loop(1, tile_count)
    def _(k):
        pl.semaphore_signal(barrier, inc=1, device_id=at_tile(lax.rem(tile + k, tile_count)), device_id_type=MESH)

    @pl.loop(1, depth_count)
    def _(k):
        pl.semaphore_signal(barrier, inc=1, device_id=(lax.rem(depth + k, depth_count), tile), device_id_type=MESH)

    across = height // BW
    lane = iota((height, breadth), 1)
    row = iota((height, breadth), 0)
    lane8 = iota((8, breadth), 1)
    row8 = iota((8, breadth), 0)
    lead = iota((across * breadth, breadth), 0) - iota((across * breadth, breadth), 1) % BW
    slot_of = iota((across * breadth, breadth), 1) // BW
    place = jnp.zeros((across * breadth, breadth), jnp.int32)
    info = jnp.zeros((8, breadth), F32)
    for s in range(HOT):
        brick = order[0, s]
        x0 = lax.rem(brick, across) * BW
        y0 = lax.div(brick, across) * BW
        dead = 1 - jnp.minimum(jnp.maximum(count[0] - s, 0), 1)
        first = lax.div(brick, across) * breadth + x0 + dead * (2 * across * breadth)
        place = jnp.where(slot_of == s, first, place)
        column = (tile * breadth + x0 + lane8 % BW).astype(F32)
        value = jnp.where(row8 == 0, y0.astype(F32), column)
        info = jnp.where(lane8 // BW == s, value, info)
    pick = jnp.where(lead == place, 1.0, 0.0).astype(BF16)
    meta[tile] = info

    heat_copy.wait()

    def pack(q):
        pieces = [
            heat[q * zq : (q + 1) * zq, m * BW : (m + 1) * BW, :].reshape(rows, breadth) for m in range(across)
        ]
        packed = jnp.dot(jnp.concatenate(pieces, axis=1), pick, preferred_element_type=F32)
        blocks[tile, q] = packed.astype(BF16)

    pack(0)
    pack(1)
    pl.semaphore_wait(barrier, tile_count + depth_count - 2)

    def part(n, sign):
        phase, slot = n // slots, lax.rem(n, slots)
        away = slot // 2
        quarter = 2 * phase + lax.rem(slot, 2) if sign < 0 else 2 * phase + 1 - lax.rem(slot, 2)
        return away, quarter

    def send(n, sign):
        away, quarter = part(n, sign)
        source = 2 * lax.rem(chip + sign * away + chips, chips) + core
        toward = 2 * lax.rem(chip - sign + chips, chips) + core
        sends, recvs = (right_send, right_recv) if sign < 0 else (left_send, left_recv)
        ref = blocks.at[source, quarter]
        return remote(ref, ref, sends.at[n], recvs.at[n], at_tile(toward))

    def arrival(n, sign):
        away, quarter = part(n, sign)
        source = lax.rem(chip + sign * (away + 1) + chips, chips)
        return source, quarter

    def received(n, sign):
        source, quarter = arrival(n, sign)
        sends, recvs = (right_send, right_recv) if sign < 0 else (left_send, left_recv)
        ref = blocks.at[2 * source + core, quarter]
        return remote(ref, ref, sends.at[n], recvs.at[n], at_tile(sibling))

    def hand_over(n, sign, mine):
        source, quarter = arrival(n, sign)
        sends, recvs = (pair_right_send, pair_right_recv) if sign < 0 else (pair_left_send, pair_left_recv)
        ref = blocks.at[2 * source + (core if mine else 1 - core), quarter]
        return remote(ref, ref, sends.at[n], recvs.at[n], at_tile(sibling))

    def own_part(q, group):
        ref = blocks.at[group, q]
        return remote(ref, ref, own_send.at[q], own_recv.at[q], at_tile(sibling))

    def meta_part(k, group):
        ref = meta.at[group]
        return remote(ref, ref, meta_send.at[k], meta_recv.at[k], at_tile(lax.rem(tile + k, tile_count)))

    def early_part(k, target, source):
        return remote(
            early_out.at[target], early_in.at[source], early_send.at[k], early_recv.at[k], (target, tile)
        )

    def late_part(k, target, source):
        return remote(late_out.at[target], late_in.at[source], late_send.at[k], late_recv.at[k], (target, tile))

    send(0, -1).start()
    send(0, 1).start()
    send(1, -1).start()
    send(1, 1).start()

    @pl.loop(1, tile_count)
    def _(k):
        meta_part(k, tile).start()

    own_part(0, tile).start()
    own_part(1, tile).start()
    pack(2)
    pack(3)
    own_part(2, tile).start()
    own_part(3, tile).start()

    offset = iota((BW, breadth), 0) - iota((BW, breadth), 1)
    turn = (offset * offset) % (2 * BW)
    chirp = jnp.cos(turn.astype(F32) * (math.pi / BW) + math.pi / 8.0)
    for s in range(height // BW):
        cosines[pl.ds(s * BW, BW), :] = chirp
    ratio_y = (row - lane).astype(F32) / (height / 4.0)
    table_y[...] = (cosines[...] / (1.0 + ratio_y * ratio_y)).astype(BF16)

    density_copy.wait()
    unit = 1.5 / (slices * depth_count)
    strip = 32

    @pl.loop(0, height // strip)
    def _(b):
        here = pl.ds(pl.multiple_of(b * strip, strip), strip)

        def slice_step(z, carry):
            total, trans, glow_sum, lit_sum = carry
            optical = density[z, here, :].astype(F32) * unit
            total = total + optical
            after = jnp.exp(-total)
            own = trans - after
            weight[z, here, :] = own
            glow_sum = glow_sum + own * heat[z, here, :].astype(F32)
            lit_sum = lit_sum + (jnp.exp(optical) - 1.0)
            return total, after, glow_sum, lit_sum

        zero = jnp.zeros((strip, breadth), F32)
        total, _, glow_sum, lit_sum = lax.fori_loop(
            0, slices, slice_step, (zero, jnp.ones_like(zero), zero, zero), unroll=4
        )
        plane[0, here, :] = glow_sum
        plane[1, here, :] = lit_sum
        high = total.astype(BF16).astype(F32)
        plane[2, here, :] = high
        plane[3, here, :] = total - high

    for d in range(depth_count):
        rows_d = [plane[p, d * band : (d + 1) * band, :] for p in range(4)]
        early_out[d] = jnp.concatenate(rows_d, axis=0).astype(BF16)

    @pl.loop(1, depth_count)
    def _(k):
        early_part(k, lax.rem(depth + k, depth_count), depth).start()

    early_in[depth] = early_out[depth]

    screen_x = (row + tile * breadth).astype(F32)
    scale = 64.0 / (HOT * tile_count * BW)

    def build(source):
        for c in range(2):
            info_c = meta[2 * source + c]
            ratio = (screen_x - info_c[1:2, :]) / (tile_count * height / 2.0)
            value = scale * (cosines[...] / (1.0 + ratio * ratio))
            for m in range(across):
                held = jnp.where(info_c[0:1, :] == float(m * BW), value, 0.0)
                tables[source, m * breadth : (m + 1) * breadth, c * breadth : (c + 1) * breadth] = held.astype(BF16)

    def product(source, q):
        left = jnp.concatenate([blocks[2 * source, q], blocks[2 * source + 1, q]], axis=1)
        return lax.dot_general(left, tables[source], (((1,), (1,)), ((), ())), preferred_element_type=F32)

    def meet(group):
        meta_part(lax.rem(tile - group + tile_count, tile_count), group).wait_recv()

    meet(sibling)
    build(chip)

    @pl.loop(0, QUARTERS)
    def _(q):
        own_part(q, sibling).wait_recv()
        spread[q] = product(chip, q)

    def collect(n):
        for sign in (-1, 1):
            hand_over(n, sign, False).wait_recv()
            source, quarter = arrival(n, sign)
            spread[quarter] += product(source, quarter)

    def finish(q, running):
        def two(i, held):
            mats = []
            for e in range(2):
                lines = spread[q, pl.ds(pl.multiple_of((2 * i + e) * BW, BW), BW), :].astype(BF16)
                mats.append(
                    jnp.concatenate([lines[:, m * breadth : (m + 1) * breadth] for m in range(across)], axis=0)
                )
            inscatter = jnp.dot(table_y[...], jnp.concatenate(mats, axis=1), preferred_element_type=F32)
            z = q * zq + 2 * i
            return held + weight[z] * inscatter[:, :breadth] + weight[z + 1] * inscatter[:, breadth:]

        return lax.fori_loop(0, zq // 2, two, running)

    plane[0] = jnp.zeros((height, breadth), F32)

    @pl.loop(0, steps)
    def _(n):
        for sign in (-1, 1):
            received(n, sign).wait_recv()

            @pl.when(n + 2 < steps)
            def _():
                send(n + 2, sign).start()

            hand_over(n, sign, True).start()

        @pl.when(n > 0)
        def _():
            collect(n - 1)

        @pl.when((n < slots) & (lax.rem(n, 2) == 0))
        def _():
            for sign in (-1, 1):
                source, _ = arrival(n, sign)

                def prepare():
                    meet(2 * source)
                    meet(2 * source + 1)
                    build(source)

                if sign < 0:
                    prepare()
                else:
                    pl.when(n < slots - 1)(prepare)

        @pl.when((n == slots + 1) | (n == slots + 2))
        def _():
            plane[0] = finish(n - slots - 1, plane[0])

        @pl.when(n == slots)
        def _():
            @pl.loop(1, depth_count)
            def _(k):
                early_part(k, depth, lax.rem(depth - k + depth_count, depth_count)).wait_recv()

            def pixel_step(k, carry):
                depth_sum, glow_sum, lit_sum = carry
                held = early_in[k].astype(F32)
                ahead = jnp.exp(-depth_sum)
                before[k] = ahead
                glow_sum = glow_sum + ahead * held[0:band]
                lit_sum = lit_sum + held[band : 2 * band]
                return depth_sum + held[2 * band : 3 * band] + held[3 * band : 4 * band], glow_sum, lit_sum

            zero = jnp.zeros((band, breadth), F32)
            depth_sum, glow_sum, lit_sum = lax.fori_loop(0, depth_count, pixel_step, (zero, zero, zero))
            passed = jnp.exp(-depth_sum)
            base[0] = glow_sum
            base[1] = lit_sum * passed
            base[2] = 1.0 - passed

    collect(steps - 1)
    running = finish(3, finish(2, plane[0]))
    for d in range(depth_count):
        late_out[d] = running[d * band : (d + 1) * band, :]

    @pl.loop(1, depth_count)
    def _(k):
        late_part(k, lax.rem(depth + k, depth_count), depth).start()

    late_in[depth] = late_out[depth]

    @pl.loop(0, steps)
    def _(n):
        for sign in (-1, 1):
            send(n, sign).wait_send()
            hand_over(n, sign, True).wait_send()

    @pl.loop(0, QUARTERS)
    def _(q):
        own_part(q, tile).wait_send()

    @pl.loop(1, tile_count)
    def _(k):
        meta_part(k, tile).wait_send()

    @pl.loop(1, depth_count)
    def _(k):
        early_part(k, lax.rem(depth + k, depth_count), depth).wait_send()

    @pl.loop(1, depth_count)
    def _(k):
        late_part(k, depth, lax.rem(depth - k + depth_count, depth_count)).wait_recv()

    scattered = lax.fori_loop(
        0, depth_count, lambda k, held: held + before[k] * late_in[k], jnp.zeros((band, breadth), F32)
    )
    lit = base[1] + scattered
    for c in range(3):
        out_ref[c] = emit[c] * base[0] + albedo[c] * lit
    out_ref[3] = base[2]

    @pl.loop(1, depth_count)
    def _(k):
        late_part(k, lax.rem(depth + k, depth_count), depth).wait_send()


def shards(density, heat, emit_color, albedo, hot_order, hot_count):
    depth_count = lax.axis_size("depth")
    tile_count = lax.axis_size("tile")
    slices, height, breadth = density.shape
    chips = tile_count // 2
    steps = 2 * (chips - 1)
    rows = slices // QUARTERS * BW
    band = height // depth_count
    across = height // BW
    dma = pltpu.SemaphoreType.DMA
    anywhere = pl.BlockSpec(memory_space=pl.ANY)
    scalars = pl.BlockSpec(memory_space=pltpu.SMEM)
    image = pl.pallas_call(
        functools.partial(render, depth_count, tile_count),
        out_shape=jax.ShapeDtypeStruct((4, band, breadth), F32),
        in_specs=[anywhere, anywhere, scalars, scalars, scalars, scalars],
        out_specs=pl.BlockSpec(memory_space=pltpu.VMEM),
        scratch_shapes=[
            pltpu.VMEM((slices, height, breadth), BF16),
            pltpu.VMEM((slices, height, breadth), BF16),
            pltpu.VMEM((slices, height, breadth), F32),
            pltpu.VMEM((tile_count, QUARTERS, rows, breadth), BF16),
            pltpu.VMEM((QUARTERS, rows, across * breadth), F32),
            pltpu.VMEM((chips, across * breadth, 2 * breadth), BF16),
            pltpu.VMEM((height, breadth), F32),
            pltpu.VMEM((height, breadth), BF16),
            pltpu.VMEM((tile_count, 8, breadth), F32),
            pltpu.VMEM((4, height, breadth), F32),
            pltpu.VMEM((depth_count, 4 * band, breadth), BF16),
            pltpu.VMEM((depth_count, 4 * band, breadth), BF16),
            pltpu.VMEM((depth_count, band, breadth), F32),
            pltpu.VMEM((depth_count, band, breadth), F32),
            pltpu.VMEM((depth_count, band, breadth), F32),
            pltpu.VMEM((3, band, breadth), F32),
            dma((2,)),
            dma((QUARTERS,)), dma((QUARTERS,)),
            dma((steps,)), dma((steps,)), dma((steps,)), dma((steps,)),
            dma((steps,)), dma((steps,)), dma((steps,)), dma((steps,)),
            dma((tile_count,)), dma((tile_count,)),
            dma((depth_count,)), dma((depth_count,)),
            dma((depth_count,)), dma((depth_count,)),
        ],
        compiler_params=pltpu.CompilerParams(
            collective_id=0, has_side_effects=True, vmem_limit_bytes=40 * 1024 * 1024
        ),
        cost_estimate=pl.CostEstimate(flops=3 * 10**9, bytes_accessed=2 * 1024 * 1024, transcendentals=10**6),
    )(density, heat, emit_color, albedo, hot_order, hot_count)
    return image.reshape(4, 1, band * breadth)


def solution(mesh):
    placed = (
        P("depth", None, "tile"),
        P("depth", None, "tile"),
        P(),
        P(),
        P("tile", None),
        P("tile"),
    )
    return jax.shard_map(
        shards, mesh=mesh, in_specs=placed, out_specs=P(None, "tile", "depth"), check_vma=False
    )
```

```python
import functools
import math

import jax
import jax.numpy as jnp
from jax import lax
from jax.experimental import pallas as pl
from jax.experimental.pallas import tpu as pltpu
from jax.sharding import PartitionSpec as P

BW = 32
HOT = 4
QUARTERS = 4
HEAD = 16
F32 = jnp.float32
BF16 = jnp.bfloat16
MESH = pl.DeviceIdType.MESH


def iota(shape, axis):
    return lax.broadcasted_iota(jnp.int32, shape, axis)


def render(
    depth_count, tile_count,
    density_hbm, heat_hbm, emit, albedo, order, count,
    out_ref,
    density, heat, weight, blocks, spread, tables, cosines, table_y, plane,
    early_out, early_in, late_out, late_in, before, base,
    heat_sem, density_sem, own_send, own_recv, right_send, right_recv, left_send, left_recv,
    pair_right_send, pair_right_recv, pair_left_send, pair_left_recv,
    early_send, early_recv, late_send, late_recv,
):
    slices, height, breadth = density.shape
    chips = tile_count // 2
    steps = 2 * (chips - 1)
    zq = slices // QUARTERS
    rows = zq * BW
    band = height // depth_count
    depth = lax.axis_index("depth")
    tile = lax.axis_index("tile")
    chip = lax.div(tile, 2)
    core = tile - 2 * chip
    sibling = 2 * chip + 1 - core

    def turned(index, count):
        return jnp.where(index >= count, index - count, index)

    ring = [turned(chip + k, chips) for k in range(chips)]

    def at_tile(index):
        return (depth, index)

    def remote(src, dst, send, recv, device):
        return pltpu.make_async_remote_copy(
            src_ref=src, dst_ref=dst, send_sem=send, recv_sem=recv, device_id=device, device_id_type=MESH
        )

    def fetch(q):
        part = pl.ds(q * zq, zq)
        return (
            pltpu.make_async_copy(heat_hbm.at[part], heat.at[part], heat_sem.at[q]),
            pltpu.make_async_copy(density_hbm.at[part], density.at[part], density_sem.at[q]),
        )

    for q in range(QUARTERS):
        fetch(q)[0].start()
    for q in range(QUARTERS):
        fetch(q)[1].start()

    barrier = pltpu.get_barrier_semaphore()

    @pl.loop(1, tile_count)
    def _(k):
        pl.semaphore_signal(barrier, inc=1, device_id=at_tile(turned(tile + k, tile_count)), device_id_type=MESH)

    @pl.loop(1, depth_count)
    def _(k):
        pl.semaphore_signal(barrier, inc=1, device_id=(turned(depth + k, depth_count), tile), device_id_type=MESH)

    across = height // BW
    lane = iota((height, breadth), 1)
    row = iota((height, breadth), 0)
    lane_h = iota((HEAD, breadth), 1)
    row_h = iota((HEAD, breadth), 0)
    lead = iota((across * breadth, breadth), 0) - iota((across * breadth, breadth), 1) % BW
    slot_of = iota((across * breadth, breadth), 1) // BW
    place = jnp.zeros((across * breadth, breadth), jnp.int32)
    info = jnp.zeros((HEAD, breadth), jnp.int32)
    for s in range(HOT):
        brick = order[0, s]
        x0 = lax.rem(brick, across) * BW
        y0 = lax.div(brick, across) * BW
        dead = 1 - jnp.minimum(jnp.maximum(count[0] - s, 0), 1)
        first = lax.div(brick, across) * breadth + x0 + dead * (2 * across * breadth)
        place = jnp.where(slot_of == s, first, place)
        value = jnp.where(row_h == 0, y0, x0 + lane_h % BW)
        info = jnp.where(lane_h // BW == s, value, info)
    pick = jnp.where(lead == place, 1.0, 0.0).astype(BF16)
    blocks[tile, 0:HEAD, :] = info.astype(F32).astype(BF16)

    def pack(q):
        fetch(q)[0].wait()
        pieces = [
            heat[q * zq : (q + 1) * zq, m * BW : (m + 1) * BW, :].reshape(rows, breadth) for m in range(across)
        ]
        packed = jnp.dot(jnp.concatenate(pieces, axis=1), pick, preferred_element_type=F32)
        blocks[tile, HEAD + q * rows : HEAD + (q + 1) * rows, :] = packed.astype(BF16)

    pack(0)
    pl.semaphore_wait(barrier, tile_count + depth_count - 2)

    half = chips // 2
    order_of = {-1: [0, 1, 2, 3] * (half - 1) + [0, 1], 1: [0, 2, 3, 1] * (half - 1) + [2, 3]}

    def lines(q):
        return pl.ds(0, HEAD + rows) if q == 0 else pl.ds(HEAD + q * rows, rows)

    def block(group, q):
        return blocks.at[group, lines(q)]

    def ring_part(n, sign, source, device):
        sends, recvs = (right_send, right_recv) if sign < 0 else (left_send, left_recv)
        ref = block(2 * source + core, order_of[sign][n])
        return remote(ref, ref, sends.at[n], recvs.at[n], at_tile(device))

    def send(n, sign):
        return ring_part(n, sign, ring[sign * (n // QUARTERS)], 2 * ring[-sign] + core)

    def arrival(n, sign):
        return ring[sign * (n // QUARTERS + 1)], order_of[sign][n]

    def received(n, sign):
        return ring_part(n, sign, arrival(n, sign)[0], sibling)

    def onward(n, sign):
        later = [m for m in range(n + 1, steps) if m // QUARTERS == n // QUARTERS + 1]
        return [m for m in later if order_of[sign][m] == order_of[sign][n]]

    def hand_over(n, sign, mine):
        source, quarter = arrival(n, sign)
        sends, recvs = (pair_right_send, pair_right_recv) if sign < 0 else (pair_left_send, pair_left_recv)
        ref = block(2 * source + (core if mine else 1 - core), quarter)
        return remote(ref, ref, sends.at[n], recvs.at[n], at_tile(sibling))

    def own_part(q, group):
        ref = block(group, q)
        return remote(ref, ref, own_send.at[q], own_recv.at[q], at_tile(sibling))

    def early_part(k, target, source):
        return remote(
            early_out.at[target], early_in.at[source], early_send.at[k], early_recv.at[k], (target, tile)
        )

    def late_part(k, target, source):
        return remote(late_out.at[target], late_in.at[source], late_send.at[k], late_recv.at[k], (target, tile))

    for q in range(QUARTERS):
        if q > 0:
            pack(q)
        for sign in (-1, 1):
            for n in range(QUARTERS):
                if max(order_of[sign][: n + 1]) == q and (order_of[sign][n] == q or n == QUARTERS - 1):
                    send(n, sign).start()
        own_part(q, tile).start()

    offset = iota((BW, breadth), 0) - iota((BW, breadth), 1)
    turn = (offset * offset) % (2 * BW)
    chirp = jnp.cos(turn.astype(F32) * (math.pi / BW) + math.pi / 8.0)
    for s in range(height // BW):
        cosines[pl.ds(s * BW, BW), :] = chirp
    ratio_y = (row - lane).astype(F32) / (height / 4.0)
    table_y[...] = (cosines[...] / (1.0 + ratio_y * ratio_y)).astype(BF16)

    for q in range(QUARTERS):
        fetch(q)[1].wait()
    unit = 1.5 / (slices * depth_count)
    strip = 32

    @pl.loop(0, height // strip)
    def _(b):
        here = pl.ds(pl.multiple_of(b * strip, strip), strip)

        def slice_step(z, carry):
            total, trans, glow_sum, lit_sum = carry
            optical = density[z, here, :].astype(F32) * unit
            total = total + optical
            after = jnp.exp(-total)
            own = trans - after
            weight[z, here, :] = own
            glow_sum = glow_sum + own * heat[z, here, :].astype(F32)
            lit_sum = lit_sum + (jnp.exp(optical) - 1.0)
            return total, after, glow_sum, lit_sum

        zero = jnp.zeros((strip, breadth), F32)
        total, _, glow_sum, lit_sum = lax.fori_loop(
            0, slices, slice_step, (zero, jnp.ones_like(zero), zero, zero), unroll=4
        )
        plane[0, here, :] = glow_sum
        plane[1, here, :] = lit_sum
        high = total.astype(BF16).astype(F32)
        plane[2, here, :] = high
        plane[3, here, :] = total - high

    for d in range(depth_count):
        rows_d = [plane[p, d * band : (d + 1) * band, :] for p in range(4)]
        early_out[d] = jnp.concatenate(rows_d, axis=0).astype(BF16)

    @pl.loop(1, depth_count)
    def _(k):
        early_part(k, turned(depth + k, depth_count), depth).start()

    early_in[depth] = early_out[depth]

    scale = 64.0 / (HOT * tile_count * BW)

    def build(source):
        for c in range(2):
            info_c = blocks[2 * source + c, 0:HEAD, :].astype(F32).T
            shift = ((tile - 2 * source - c) * breadth).astype(F32)
            ratio = (lane.astype(F32) + shift - info_c[:, 1:2]) / (tile_count * height / 2.0)
            value = scale * (cosines[...] / (1.0 + ratio * ratio))
            for m in range(across):
                held = jnp.where(info_c[:, 0:1] == float(m * BW), value, 0.0)
                tables[source, c * breadth : (c + 1) * breadth, m * breadth : (m + 1) * breadth] = held.astype(BF16)

    def product(source, q):
        part = slice(HEAD + q * rows, HEAD + (q + 1) * rows)
        left = jnp.concatenate([blocks[2 * source, part, :], blocks[2 * source + 1, part, :]], axis=1)
        return jnp.dot(left, tables[source], preferred_element_type=F32)

    own_part(0, sibling).wait_recv()
    build(chip)
    spread[0] = product(chip, 0)
    for q in range(1, QUARTERS):
        own_part(q, sibling).wait_recv()
        spread[q] = product(chip, q)

    def collect(n):
        for sign in (-1, 1):
            hand_over(n, sign, False).wait_recv()
        for sign in (-1, 1):
            source, quarter = arrival(n, sign)
            if quarter == 0:
                build(source)
            spread[quarter] += product(source, quarter)

    def finish(q, running):
        mats = []
        for z in range(zq):
            flat = spread[q, z * BW : (z + 1) * BW, :].astype(BF16)
            mats.append(jnp.concatenate([flat[:, m * breadth : (m + 1) * breadth] for m in range(across)], axis=0))
        inscatter = jnp.dot(table_y[...], jnp.concatenate(mats, axis=1), preferred_element_type=F32)
        for z in range(zq):
            running = running + weight[q * zq + z] * inscatter[:, z * breadth : (z + 1) * breadth]
        return running

    def gather_early():
        @pl.loop(1, depth_count)
        def _(k):
            early_part(k, depth, turned(depth - k + depth_count, depth_count)).wait_recv()

        def pixel_step(k, carry):
            depth_sum, glow_sum, lit_sum = carry
            held = early_in[k].astype(F32)
            ahead = jnp.exp(-depth_sum)
            before[k] = ahead
            glow_sum = glow_sum + ahead * held[0:band]
            lit_sum = lit_sum + held[band : 2 * band]
            return depth_sum + held[2 * band : 3 * band] + held[3 * band : 4 * band], glow_sum, lit_sum

        zero = jnp.zeros((band, breadth), F32)
        depth_sum, glow_sum, lit_sum = lax.fori_loop(0, depth_count, pixel_step, (zero, zero, zero))
        passed = jnp.exp(-depth_sum)
        base[0] = glow_sum
        base[1] = lit_sum * passed
        base[2] = 1.0 - passed

    for n in range(steps):
        for sign in (-1, 1):
            received(n, sign).wait_recv()
            for m in onward(n, sign):
                send(m, sign).start()
            hand_over(n, sign, True).start()
        if n > 0:
            collect(n - 1)
        if n == 2 * half:
            gather_early()

    running = finish(2, finish(0, jnp.zeros((height, breadth), F32)))
    collect(steps - 1)
    running = finish(3, finish(1, running))
    for d in range(depth_count):
        late_out[d] = running[d * band : (d + 1) * band, :]

    @pl.loop(1, depth_count)
    def _(k):
        late_part(k, turned(depth + k, depth_count), depth).start()

    late_in[depth] = late_out[depth]

    for n in range(steps):
        for sign in (-1, 1):
            send(n, sign).wait_send()
            hand_over(n, sign, True).wait_send()

    for q in range(QUARTERS):
        own_part(q, tile).wait_send()

    @pl.loop(1, depth_count)
    def _(k):
        early_part(k, turned(depth + k, depth_count), depth).wait_send()

    @pl.loop(1, depth_count)
    def _(k):
        late_part(k, depth, turned(depth - k + depth_count, depth_count)).wait_recv()

    scattered = lax.fori_loop(
        0, depth_count, lambda k, held: held + before[k] * late_in[k], jnp.zeros((band, breadth), F32)
    )
    lit = base[1] + scattered
    for c in range(3):
        out_ref[c] = emit[c] * base[0] + albedo[c] * lit
    out_ref[3] = base[2]

    @pl.loop(1, depth_count)
    def _(k):
        late_part(k, turned(depth + k, depth_count), depth).wait_send()


def shards(density, heat, emit_color, albedo, hot_order, hot_count):
    depth_count = lax.axis_size("depth")
    tile_count = lax.axis_size("tile")
    slices, height, breadth = density.shape
    chips = tile_count // 2
    steps = 2 * (chips - 1)
    rows = slices // QUARTERS * BW
    band = height // depth_count
    across = height // BW
    dma = pltpu.SemaphoreType.DMA
    anywhere = pl.BlockSpec(memory_space=pltpu.HBM)
    scalars = pl.BlockSpec(memory_space=pltpu.SMEM)
    image = pl.pallas_call(
        functools.partial(render, depth_count, tile_count),
        out_shape=jax.ShapeDtypeStruct((4, band, breadth), F32),
        in_specs=[anywhere, anywhere, scalars, scalars, scalars, scalars],
        out_specs=pl.BlockSpec(memory_space=pltpu.VMEM),
        scratch_shapes=[
            pltpu.VMEM((slices, height, breadth), BF16),
            pltpu.VMEM((slices, height, breadth), BF16),
            pltpu.VMEM((slices, height, breadth), F32),
            pltpu.VMEM((tile_count, HEAD + slices * BW, breadth), BF16),
            pltpu.VMEM((QUARTERS, rows, across * breadth), F32),
            pltpu.VMEM((chips, 2 * breadth, across * breadth), BF16),
            pltpu.VMEM((height, breadth), F32),
            pltpu.VMEM((height, breadth), BF16),
            pltpu.VMEM((4, height, breadth), F32),
            pltpu.VMEM((depth_count, 4 * band, breadth), BF16),
            pltpu.VMEM((depth_count, 4 * band, breadth), BF16),
            pltpu.VMEM((depth_count, band, breadth), F32),
            pltpu.VMEM((depth_count, band, breadth), F32),
            pltpu.VMEM((depth_count, band, breadth), F32),
            pltpu.VMEM((3, band, breadth), F32),
            dma((QUARTERS,)), dma((QUARTERS,)),
            dma((QUARTERS,)), dma((QUARTERS,)),
            dma((steps,)), dma((steps,)), dma((steps,)), dma((steps,)),
            dma((steps,)), dma((steps,)), dma((steps,)), dma((steps,)),
            dma((depth_count,)), dma((depth_count,)),
            dma((depth_count,)), dma((depth_count,)),
        ],
        compiler_params=pltpu.CompilerParams(
            collective_id=0, has_side_effects=True, vmem_limit_bytes=60 * 1024 * 1024
        ),
        cost_estimate=pl.CostEstimate(flops=3 * 10**9, bytes_accessed=2 * 1024 * 1024, transcendentals=10**6),
    )(density, heat, emit_color, albedo, hot_order, hot_count)
    return image.reshape(4, 1, band * breadth)


def solution(mesh):
    placed = (
        P("depth", None, "tile"),
        P("depth", None, "tile"),
        P(),
        P(),
        P("tile", None),
        P("tile"),
    )
    return jax.shard_map(
        shards, mesh=mesh, in_specs=placed, out_specs=P(None, "tile", "depth"), check_vma=False
    )
```

```python
import functools
import math

import jax
import jax.numpy as jnp
from jax import lax
from jax.experimental import pallas as pl
from jax.experimental.pallas import tpu as pltpu
from jax.sharding import PartitionSpec as P

BW = 32
HOT = 4
QUARTERS = 4
HEAD = 16
COLUMNS = 4
F32 = jnp.float32
BF16 = jnp.bfloat16
MESH = pl.DeviceIdType.MESH


def iota(shape, axis):
    return lax.broadcasted_iota(jnp.int32, shape, axis)


def render(
    depth_count, tile_count,
    density_hbm, heat_hbm, emit_hbm, albedo_hbm, order_hbm, count_hbm,
    out_ref,
    emit, albedo, order, count, density, heat, weight, blocks, spread, tables, cosines, table_y, plane,
    early_out, early_in, late_out, late_in, before, base,
    scalar_sem, heat_sem, density_sem, own_send, own_recv, right_send, right_recv, left_send, left_recv,
    pair_right_send, pair_right_recv, pair_left_send, pair_left_recv,
    early_send, early_recv, late_send, late_recv, word,
):
    slices, height, breadth = density.shape
    chips = tile_count // 2
    steps = 2 * (chips - 1)
    zq = slices // QUARTERS
    rows = zq * BW
    band = height // depth_count
    depth = lax.axis_index("depth")
    tile = lax.axis_index("tile")
    chip = lax.div(tile, 2)
    core = tile - 2 * chip
    sibling = 2 * chip + 1 - core

    def turned(index, count):
        return jnp.where(index >= count, index - count, index)

    ring = [turned(chip + k, chips) for k in range(chips)]
    columns = min(COLUMNS, depth_count)
    planes = depth_count // columns
    z_here = lax.div(depth, columns)
    x_here = depth - z_here * columns
    z_ring = [turned(z_here + k, planes) for k in range(planes)]
    x_ring = [turned(x_here + k, columns) for k in range(columns)]

    def beside(size):
        return [1, size - 1] if size > 2 else [1] * (size - 1)

    x_beside = [(z_here * columns + x_ring[k], tile) for k in beside(columns)]
    z_beside = [(z_ring[k] * columns + x_here, tile) for k in beside(planes)]
    far_first = sorted(
        [(a, b) for a in range(planes) for b in range(columns) if a + b],
        key=lambda e: -min(e[0], planes - e[0]) - min(e[1], columns - e[1]),
    )

    def partner(a, b):
        return z_ring[a] * columns + x_ring[b]

    def at_tile(index):
        return (depth, index)

    def remote(src, dst, send, recv, device):
        return pltpu.make_async_remote_copy(
            src_ref=src, dst_ref=dst, send_sem=send, recv_sem=recv, device_id=device, device_id_type=MESH
        )

    def fetch(q):
        part = pl.ds(q * zq, zq)
        return (
            pltpu.make_async_copy(heat_hbm.at[part], heat.at[part], heat_sem.at[q]),
            pltpu.make_async_copy(density_hbm.at[part], density.at[part], density_sem.at[q]),
        )

    scalars = [(order_hbm, order), (count_hbm, count), (emit_hbm, emit), (albedo_hbm, albedo)]
    loads = [pltpu.make_async_copy(src, dst, scalar_sem.at[i]) for i, (src, dst) in enumerate(scalars)]
    loads[0].start()
    loads[1].start()
    fetch(0)[0].start()

    barrier = pltpu.get_barrier_semaphore()

    greeted = [(depth, 2 * ring[1] + core), (depth, 2 * ring[-1] + core), (depth, sibling)] + x_beside + z_beside
    for device in greeted:
        pl.semaphore_signal(barrier, inc=1, device_id=device, device_id_type=MESH)

    for q in range(1, QUARTERS):
        fetch(q)[0].start()
    for q in range(QUARTERS):
        fetch(q)[1].start()
    loads[2].start()
    loads[3].start()

    rounds = [x_beside] * (columns // 2 - 1) + [z_beside] * (planes // 2)

    def pass_word(r):
        if 0 < r <= len(rounds):
            pl.semaphore_wait(word.at[r - 1], len(rounds[r - 1]))
        if r < len(rounds):
            for device in rounds[r]:
                pl.semaphore_signal(word.at[r], inc=1, device_id=device, device_id_type=MESH)

    across = height // BW
    lane = iota((height, breadth), 1)
    row = iota((height, breadth), 0)
    lane_h = iota((HEAD, breadth), 1)
    row_h = iota((HEAD, breadth), 0)
    lead = iota((across * breadth, breadth), 0) - iota((across * breadth, breadth), 1) % BW
    slot_of = iota((across * breadth, breadth), 1) // BW
    place = jnp.zeros((across * breadth, breadth), jnp.int32)
    info = jnp.zeros((HEAD, breadth), jnp.int32)
    loads[0].wait()
    loads[1].wait()
    for s in range(HOT):
        brick = order[0, s]
        x0 = lax.rem(brick, across) * BW
        y0 = lax.div(brick, across) * BW
        dead = 1 - jnp.minimum(jnp.maximum(count[0] - s, 0), 1)
        first = lax.div(brick, across) * breadth + x0 + dead * (2 * across * breadth)
        place = jnp.where(slot_of == s, first, place)
        value = jnp.where(row_h == 0, y0, x0 + lane_h % BW)
        info = jnp.where(lane_h // BW == s, value, info)
    pick = jnp.where(lead == place, 1.0, 0.0).astype(BF16)
    blocks[tile, 0:HEAD, :] = info.astype(F32).astype(BF16)

    def pack(q):
        fetch(q)[0].wait()
        pieces = [
            heat[q * zq : (q + 1) * zq, m * BW : (m + 1) * BW, :].reshape(rows, breadth) for m in range(across)
        ]
        packed = jnp.dot(jnp.concatenate(pieces, axis=1), pick, preferred_element_type=F32)
        blocks[tile, HEAD + q * rows : HEAD + (q + 1) * rows, :] = packed.astype(BF16)

    pack(0)
    pl.semaphore_wait(barrier, len(greeted))

    half = chips // 2
    order_of = {-1: [0, 1, 2, 3] * (half - 1) + [0, 1], 1: [0, 2, 3, 1] * (half - 1) + [2, 3]}

    def lines(q):
        return pl.ds(0, HEAD + rows) if q == 0 else pl.ds(HEAD + q * rows, rows)

    def block(group, q):
        return blocks.at[group, lines(q)]

    def ring_part(n, sign, source, device):
        sends, recvs = (right_send, right_recv) if sign < 0 else (left_send, left_recv)
        ref = block(2 * source + core, order_of[sign][n])
        return remote(ref, ref, sends.at[n], recvs.at[n], at_tile(device))

    def send(n, sign):
        return ring_part(n, sign, ring[sign * (n // QUARTERS)], 2 * ring[-sign] + core)

    def arrival(n, sign):
        return ring[sign * (n // QUARTERS + 1)], order_of[sign][n]

    def received(n, sign):
        return ring_part(n, sign, arrival(n, sign)[0], sibling)

    def onward(n, sign):
        later = [m for m in range(n + 1, steps) if m // QUARTERS == n // QUARTERS + 1]
        return [m for m in later if order_of[sign][m] == order_of[sign][n]]

    def hand_over(n, sign, mine):
        source, quarter = arrival(n, sign)
        sends, recvs = (pair_right_send, pair_right_recv) if sign < 0 else (pair_left_send, pair_left_recv)
        ref = block(2 * source + (core if mine else 1 - core), quarter)
        return remote(ref, ref, sends.at[n], recvs.at[n], at_tile(sibling))

    def own_part(q, group):
        ref = block(group, q)
        return remote(ref, ref, own_send.at[q], own_recv.at[q], at_tile(sibling))

    def early_part(a, b, target, source):
        k = a * columns + b
        return remote(
            early_out.at[target], early_in.at[source], early_send.at[k], early_recv.at[k], (target, tile)
        )

    def late_part(a, b, target, source):
        k = a * columns + b
        return remote(late_out.at[target], late_in.at[source], late_send.at[k], late_recv.at[k], (target, tile))

    def leaving(part, a, b):
        return part(a, b, partner(a, b), depth)

    def coming(part, a, b):
        return part(a, b, depth, partner(-a, -b))

    for q in range(QUARTERS):
        if q > 0:
            pack(q)
        for sign in (-1, 1):
            for n in range(QUARTERS):
                if max(order_of[sign][: n + 1]) == q and (order_of[sign][n] == q or n == QUARTERS - 1):
                    send(n, sign).start()
        own_part(q, tile).start()
    pass_word(0)

    offset = iota((BW, breadth), 0) - iota((BW, breadth), 1)
    turn = (offset * offset) % (2 * BW)
    chirp = jnp.cos(turn.astype(F32) * (math.pi / BW) + math.pi / 8.0)
    for s in range(height // BW):
        cosines[pl.ds(s * BW, BW), :] = chirp
    ratio_y = (row - lane).astype(F32) / (height / 4.0)
    table_y[...] = (cosines[...] / (1.0 + ratio_y * ratio_y)).astype(BF16)

    for q in range(QUARTERS):
        fetch(q)[1].wait()
    unit = 1.5 / (slices * depth_count)
    strip = 32

    @pl.loop(0, height // strip)
    def _(b):
        here = pl.ds(pl.multiple_of(b * strip, strip), strip)

        def slice_step(z, carry):
            total, trans, glow_sum, lit_sum = carry
            optical = density[z, here, :].astype(F32) * unit
            total = total + optical
            after = jnp.exp(-total)
            own = trans - after
            weight[z, here, :] = own
            glow_sum = glow_sum + own * heat[z, here, :].astype(F32)
            lit_sum = lit_sum + (jnp.exp(optical) - 1.0)
            return total, after, glow_sum, lit_sum

        zero = jnp.zeros((strip, breadth), F32)
        total, _, glow_sum, lit_sum = lax.fori_loop(
            0, slices, slice_step, (zero, jnp.ones_like(zero), zero, zero), unroll=4
        )
        plane[0, here, :] = glow_sum
        plane[1, here, :] = lit_sum
        high = total.astype(BF16).astype(F32)
        plane[2, here, :] = high
        plane[3, here, :] = total - high

    for d in range(depth_count):
        rows_d = [plane[p, d * band : (d + 1) * band, :] for p in range(4)]
        early_out[d] = jnp.concatenate(rows_d, axis=0).astype(BF16)

    early_in[depth] = early_out[depth]

    scale = 64.0 / (HOT * tile_count * BW)

    def build(source):
        for c in range(2):
            info_c = blocks[2 * source + c, 0:HEAD, :].astype(F32).T
            shift = ((tile - 2 * source - c) * breadth).astype(F32)
            ratio = (lane.astype(F32) + shift - info_c[:, 1:2]) / (tile_count * height / 2.0)
            value = scale * (cosines[...] / (1.0 + ratio * ratio))
            for m in range(across):
                held = jnp.where(info_c[:, 0:1] == float(m * BW), value, 0.0)
                tables[source, c * breadth : (c + 1) * breadth, m * breadth : (m + 1) * breadth] = held.astype(BF16)

    def product(source, q):
        part = slice(HEAD + q * rows, HEAD + (q + 1) * rows)
        left = jnp.concatenate([blocks[2 * source, part, :], blocks[2 * source + 1, part, :]], axis=1)
        return jnp.dot(left, tables[source], preferred_element_type=F32)

    own_part(0, sibling).wait_recv()
    build(chip)
    spread[0] = product(chip, 0)
    for q in range(1, QUARTERS):
        own_part(q, sibling).wait_recv()
        spread[q] = product(chip, q)

    def collect(n):
        for sign in (-1, 1):
            hand_over(n, sign, False).wait_recv()
        for sign in (-1, 1):
            source, quarter = arrival(n, sign)
            if quarter == 0:
                build(source)
            spread[quarter] += product(source, quarter)

    def finish(q, running):
        mats = []
        for z in range(zq):
            flat = spread[q, z * BW : (z + 1) * BW, :].astype(BF16)
            mats.append(jnp.concatenate([flat[:, m * breadth : (m + 1) * breadth] for m in range(across)], axis=0))
        inscatter = jnp.dot(table_y[...], jnp.concatenate(mats, axis=1), preferred_element_type=F32)
        for z in range(zq):
            running = running + weight[q * zq + z] * inscatter[:, z * breadth : (z + 1) * breadth]
        return running

    def gather_early():
        for a, b in far_first:
            coming(early_part, a, b).wait_recv()

        def pixel_step(k, carry):
            depth_sum, glow_sum, lit_sum = carry
            held = early_in[k].astype(F32)
            ahead = jnp.exp(-depth_sum)
            before[k] = ahead
            glow_sum = glow_sum + ahead * held[0:band]
            lit_sum = lit_sum + held[band : 2 * band]
            return depth_sum + held[2 * band : 3 * band] + held[3 * band : 4 * band], glow_sum, lit_sum

        zero = jnp.zeros((band, breadth), F32)
        depth_sum, glow_sum, lit_sum = lax.fori_loop(0, depth_count, pixel_step, (zero, zero, zero))
        passed = jnp.exp(-depth_sum)
        base[0] = glow_sum
        base[1] = lit_sum * passed
        base[2] = 1.0 - passed

    for n in range(steps):
        for sign in (-1, 1):
            received(n, sign).wait_recv()
            for m in onward(n, sign):
                send(m, sign).start()
            hand_over(n, sign, True).start()
        if n > 0:
            collect(n - 1)
        pass_word(n + 1)
        if n + 1 == max(len(rounds), 1):
            for a, b in far_first:
                leaving(early_part, a, b).start()
        if n == steps - 4:
            gather_early()

    running = finish(2, finish(0, jnp.zeros((height, breadth), F32)))
    collect(steps - 1)
    running = finish(3, finish(1, running))
    for d in range(depth_count):
        late_out[d] = running[d * band : (d + 1) * band, :]

    for a, b in far_first:
        leaving(late_part, a, b).start()

    late_in[depth] = late_out[depth]

    for n in range(steps):
        for sign in (-1, 1):
            send(n, sign).wait_send()
            hand_over(n, sign, True).wait_send()

    for q in range(QUARTERS):
        own_part(q, tile).wait_send()

    for a, b in far_first:
        leaving(early_part, a, b).wait_send()
    for a, b in far_first:
        coming(late_part, a, b).wait_recv()

    scattered = lax.fori_loop(
        0, depth_count, lambda k, held: held + before[k] * late_in[k], jnp.zeros((band, breadth), F32)
    )
    loads[2].wait()
    loads[3].wait()
    lit = base[1] + scattered
    for c in range(3):
        out_ref[c] = emit[c] * base[0] + albedo[c] * lit
    out_ref[3] = base[2]

    for a, b in far_first:
        leaving(late_part, a, b).wait_send()


def shards(density, heat, emit_color, albedo, hot_order, hot_count):
    depth_count = lax.axis_size("depth")
    tile_count = lax.axis_size("tile")
    slices, height, breadth = density.shape
    chips = tile_count // 2
    steps = 2 * (chips - 1)
    rows = slices // QUARTERS * BW
    band = height // depth_count
    across = height // BW
    dma = pltpu.SemaphoreType.DMA
    anywhere = pl.BlockSpec(memory_space=pl.ANY)
    image = pl.pallas_call(
        functools.partial(render, depth_count, tile_count),
        out_shape=jax.ShapeDtypeStruct((4, band, breadth), F32),
        in_specs=[anywhere] * 6,
        out_specs=pl.BlockSpec(memory_space=pltpu.VMEM),
        scratch_shapes=[
            pltpu.SMEM((3,), F32), pltpu.SMEM((3,), F32), pltpu.SMEM((1, 16), jnp.int32), pltpu.SMEM((1,), jnp.int32),
            pltpu.VMEM((slices, height, breadth), BF16),
            pltpu.VMEM((slices, height, breadth), BF16),
            pltpu.VMEM((slices, height, breadth), F32),
            pltpu.VMEM((tile_count, HEAD + slices * BW, breadth), BF16),
            pltpu.VMEM((QUARTERS, rows, across * breadth), F32),
            pltpu.VMEM((chips, 2 * breadth, across * breadth), BF16),
            pltpu.VMEM((height, breadth), F32),
            pltpu.VMEM((height, breadth), BF16),
            pltpu.VMEM((4, height, breadth), F32),
            pltpu.VMEM((depth_count, 4 * band, breadth), BF16),
            pltpu.VMEM((depth_count, 4 * band, breadth), BF16),
            pltpu.VMEM((depth_count, band, breadth), F32),
            pltpu.VMEM((depth_count, band, breadth), F32),
            pltpu.VMEM((depth_count, band, breadth), F32),
            pltpu.VMEM((3, band, breadth), F32),
            dma((4,)), dma((QUARTERS,)), dma((QUARTERS,)),
            dma((QUARTERS,)), dma((QUARTERS,)),
            dma((steps,)), dma((steps,)), dma((steps,)), dma((steps,)),
            dma((steps,)), dma((steps,)), dma((steps,)), dma((steps,)),
            dma((depth_count,)), dma((depth_count,)),
            dma((depth_count,)), dma((depth_count,)),
            pltpu.SemaphoreType.REGULAR((8,)),
        ],
        compiler_params=pltpu.CompilerParams(
            collective_id=0, has_side_effects=True, vmem_limit_bytes=54400 * 1024
        ),
        cost_estimate=pl.CostEstimate(flops=3 * 10**9, bytes_accessed=2 * 1024 * 1024, transcendentals=10**6),
    )(density, heat, emit_color, albedo, hot_order, hot_count)
    return image.reshape(4, 1, band * breadth)


def solution(mesh):
    placed = (
        P("depth", None, "tile"),
        P("depth", None, "tile"),
        P(),
        P(),
        P("tile", None),
        P("tile"),
    )
    return jax.shard_map(
        shards, mesh=mesh, in_specs=placed, out_specs=P(None, "tile", "depth"), check_vma=False
    )
```

```python
import functools
import math

import jax
import jax.numpy as jnp
from jax import lax
from jax.experimental import pallas as pl
from jax.experimental.pallas import tpu as pltpu
from jax.sharding import PartitionSpec as P

BW = 32
HOT = 4
QUARTERS = 4
HEAD = 16
COLUMNS = 4
BEHIND = 4
F32 = jnp.float32
BF16 = jnp.bfloat16
MESH = pl.DeviceIdType.MESH


def iota(shape, axis):
    return lax.broadcasted_iota(jnp.int32, shape, axis)


def render(
    depth_count, tile_count,
    density_hbm, heat_hbm, emit_hbm, albedo_hbm, order_hbm, count_hbm,
    out_ref,
    emit, albedo, order, count, density, heat, weight, blocks, spread, tables, cosines, table_y, plane,
    early_out, early_in, late_out, late_in, before, base,
    scalar_sem, heat_sem, density_sem, own_send, own_recv, right_send, right_recv, left_send, left_recv,
    pair_right_send, pair_right_recv, pair_left_send, pair_left_recv,
    early_send, early_recv, late_send, late_recv, word,
):
    slices, height, breadth = density.shape
    chips = tile_count // 2
    steps = 2 * (chips - 1)
    zq = slices // QUARTERS
    rows = zq * BW
    band = height // depth_count
    depth = lax.axis_index("depth")
    tile = lax.axis_index("tile")
    chip = lax.div(tile, 2)
    core = tile - 2 * chip
    sibling = 2 * chip + 1 - core

    def turned(index, count):
        return jnp.where(index >= count, index - count, index)

    ring = [turned(chip + k, chips) for k in range(chips)]
    columns = min(COLUMNS, depth_count)
    planes = depth_count // columns
    z_here = lax.div(depth, columns)
    x_here = depth - z_here * columns
    z_ring = [turned(z_here + k, planes) for k in range(planes)]
    x_ring = [turned(x_here + k, columns) for k in range(columns)]

    def beside(size):
        return [1, size - 1] if size > 2 else [1] * (size - 1)

    x_beside = [(z_here * columns + x_ring[k], tile) for k in beside(columns)]
    z_beside = [(z_ring[k] * columns + x_here, tile) for k in beside(planes)]
    far_first = sorted(
        [(a, b) for a in range(planes) for b in range(columns) if a + b],
        key=lambda e: -min(e[0], planes - e[0]) - min(e[1], columns - e[1]),
    )

    def partner(a, b):
        return z_ring[a] * columns + x_ring[b]

    def at_tile(index):
        return (depth, index)

    def remote(src, dst, send, recv, device):
        return pltpu.make_async_remote_copy(
            src_ref=src, dst_ref=dst, send_sem=send, recv_sem=recv, device_id=device, device_id_type=MESH
        )

    def fetch(q):
        part = pl.ds(q * zq, zq)
        return (
            pltpu.make_async_copy(heat_hbm.at[part], heat.at[part], heat_sem.at[q]),
            pltpu.make_async_copy(density_hbm.at[part], density.at[part], density_sem.at[q]),
        )

    scalars = [(order_hbm, order), (count_hbm, count), (emit_hbm, emit), (albedo_hbm, albedo)]
    loads = [pltpu.make_async_copy(src, dst, scalar_sem.at[i]) for i, (src, dst) in enumerate(scalars)]
    loads[0].start()
    loads[1].start()
    fetch(0)[0].start()

    barrier = pltpu.get_barrier_semaphore()

    greeted = [(depth, 2 * ring[1] + core), (depth, 2 * ring[-1] + core), (depth, sibling)] + x_beside + z_beside
    for device in greeted:
        pl.semaphore_signal(barrier, inc=1, device_id=device, device_id_type=MESH)

    for q in range(1, QUARTERS):
        fetch(q)[0].start()
    for q in range(QUARTERS):
        fetch(q)[1].start()
    loads[2].start()
    loads[3].start()

    rounds = [x_beside] * (columns // 2 - 1) + [z_beside] * (planes // 2)

    def pass_word(r):
        if 0 < r <= len(rounds):
            pl.semaphore_wait(word.at[r - 1], len(rounds[r - 1]))
        if r < len(rounds):
            for device in rounds[r]:
                pl.semaphore_signal(word.at[r], inc=1, device_id=device, device_id_type=MESH)

    across = height // BW
    lane = iota((height, breadth), 1)
    row = iota((height, breadth), 0)
    lane_h = iota((HEAD, breadth), 1)
    row_h = iota((HEAD, breadth), 0)
    lead = iota((across * breadth, breadth), 0) - iota((across * breadth, breadth), 1) % BW
    slot_of = iota((across * breadth, breadth), 1) // BW
    place = jnp.zeros((across * breadth, breadth), jnp.int32)
    info = jnp.zeros((HEAD, breadth), jnp.int32)
    loads[0].wait()
    loads[1].wait()
    for s in range(HOT):
        brick = order[0, s]
        x0 = lax.rem(brick, across) * BW
        y0 = lax.div(brick, across) * BW
        dead = 1 - jnp.minimum(jnp.maximum(count[0] - s, 0), 1)
        first = lax.div(brick, across) * breadth + x0 + dead * (2 * across * breadth)
        place = jnp.where(slot_of == s, first, place)
        value = jnp.where(row_h == 0, y0, x0 + lane_h % BW)
        info = jnp.where(lane_h // BW == s, value, info)
    pick = jnp.where(lead == place, 1.0, 0.0).astype(BF16)
    blocks[tile, 0:HEAD, :] = info.astype(F32).astype(BF16)

    def pack(q):
        fetch(q)[0].wait()
        pieces = [
            heat[q * zq : (q + 1) * zq, m * BW : (m + 1) * BW, :].reshape(rows, breadth) for m in range(across)
        ]
        packed = jnp.dot(jnp.concatenate(pieces, axis=1), pick, preferred_element_type=F32)
        blocks[tile, HEAD + q * rows : HEAD + (q + 1) * rows, :] = packed.astype(BF16)

    pack(0)
    pl.semaphore_wait(barrier, len(greeted))

    half = chips // 2
    order_of = {-1: [0, 1, 2, 3] * (half - 1) + [0, 1], 1: [0, 2, 3, 1] * (half - 1) + [2, 3]}

    def lines(q):
        return pl.ds(0, HEAD + rows) if q == 0 else pl.ds(HEAD + q * rows, rows)

    def block(group, q):
        return blocks.at[group, lines(q)]

    def ring_part(n, sign, source, device):
        sends, recvs = (right_send, right_recv) if sign < 0 else (left_send, left_recv)
        ref = block(2 * source + core, order_of[sign][n])
        return remote(ref, ref, sends.at[n], recvs.at[n], at_tile(device))

    def send(n, sign):
        return ring_part(n, sign, ring[sign * (n // QUARTERS)], 2 * ring[-sign] + core)

    def arrival(n, sign):
        return ring[sign * (n // QUARTERS + 1)], order_of[sign][n]

    def received(n, sign):
        return ring_part(n, sign, arrival(n, sign)[0], sibling)

    def onward(n, sign):
        later = [m for m in range(n + 1, steps) if m // QUARTERS == n // QUARTERS + 1]
        return [m for m in later if order_of[sign][m] == order_of[sign][n]]

    def hand_over(n, sign, mine):
        source, quarter = arrival(n, sign)
        sends, recvs = (pair_right_send, pair_right_recv) if sign < 0 else (pair_left_send, pair_left_recv)
        ref = block(2 * source + (core if mine else 1 - core), quarter)
        return remote(ref, ref, sends.at[n], recvs.at[n], at_tile(sibling))

    def own_part(q, group):
        ref = block(group, q)
        return remote(ref, ref, own_send.at[q], own_recv.at[q], at_tile(sibling))

    def early_part(target, source):
        return remote(early_out.at[target], early_in.at[source], early_send, early_recv, (target, tile))

    def late_part(target, source):
        return remote(late_out.at[target], late_in.at[source], late_send, late_recv, (target, tile))

    def leaving(part, a, b):
        return part(partner(a, b), depth)

    def everyone(out, into, send_sem, recv_sem):
        others = pl.ds(0, depth_count - 1)
        return remote(out.at[others], into.at[others], send_sem, recv_sem, (depth, sibling))

    early_all = everyone(early_out, early_in, early_send, early_recv)
    late_all = everyone(late_out, late_in, late_send, late_recv)

    for q in range(QUARTERS):
        if q > 0:
            pack(q)
        for sign in (-1, 1):
            for n in range(QUARTERS):
                if max(order_of[sign][: n + 1]) == q and (order_of[sign][n] == q or n == QUARTERS - 1):
                    send(n, sign).start()
        own_part(q, tile).start()
    pass_word(0)

    offset = iota((BW, breadth), 0) - iota((BW, breadth), 1)
    turn = (offset * offset) % (2 * BW)
    chirp = jnp.cos(turn.astype(F32) * (math.pi / BW) + math.pi / 8.0)
    for s in range(height // BW):
        cosines[pl.ds(s * BW, BW), :] = chirp
    ratio_y = (row - lane).astype(F32) / (height / 4.0)
    table_y[...] = (cosines[...] / (1.0 + ratio_y * ratio_y)).astype(BF16)

    for q in range(QUARTERS):
        fetch(q)[1].wait()
    unit = 1.5 / (slices * depth_count)
    strip = 32

    @pl.loop(0, height // strip)
    def _(b):
        here = pl.ds(pl.multiple_of(b * strip, strip), strip)

        def slice_step(z, carry):
            total, trans, glow_sum, lit_sum = carry
            optical = density[z, here, :].astype(F32) * unit
            total = total + optical
            after = jnp.exp(-total)
            own = trans - after
            weight[z, here, :] = own
            glow_sum = glow_sum + own * heat[z, here, :].astype(F32)
            lit_sum = lit_sum + (jnp.exp(optical) - 1.0)
            return total, after, glow_sum, lit_sum

        zero = jnp.zeros((strip, breadth), F32)
        total, _, glow_sum, lit_sum = lax.fori_loop(
            0, slices, slice_step, (zero, jnp.ones_like(zero), zero, zero), unroll=4
        )
        plane[0, here, :] = glow_sum
        plane[1, here, :] = lit_sum
        high = total.astype(BF16).astype(F32)
        plane[2, here, :] = high
        plane[3, here, :] = total - high

    for d in range(depth_count):
        rows_d = [plane[p, d * band : (d + 1) * band, :] for p in range(4)]
        early_out[d] = jnp.concatenate(rows_d, axis=0).astype(BF16)

    early_in[depth] = early_out[depth]

    scale = 64.0 / (HOT * tile_count * BW)

    def build(source):
        for c in range(2):
            info_c = blocks[2 * source + c, 0:HEAD, :].astype(F32).T
            shift = ((tile - 2 * source - c) * breadth).astype(F32)
            ratio = (lane.astype(F32) + shift - info_c[:, 1:2]) / (tile_count * height / 2.0)
            value = scale * (cosines[...] / (1.0 + ratio * ratio))
            for m in range(across):
                held = jnp.where(info_c[:, 0:1] == float(m * BW), value, 0.0)
                tables[source, c * breadth : (c + 1) * breadth, m * breadth : (m + 1) * breadth] = held.astype(BF16)

    def product(source, q):
        part = slice(HEAD + q * rows, HEAD + (q + 1) * rows)
        left = jnp.concatenate([blocks[2 * source, part, :], blocks[2 * source + 1, part, :]], axis=1)
        return jnp.dot(left, tables[source], preferred_element_type=F32)

    own_part(0, sibling).wait_recv()
    build(chip)
    spread[0] = product(chip, 0)
    for q in range(1, QUARTERS):
        own_part(q, sibling).wait_recv()
        spread[q] = product(chip, q)

    def collect(n):
        for sign in (-1, 1):
            hand_over(n, sign, False).wait_recv()
        for sign in (-1, 1):
            source, quarter = arrival(n, sign)
            if quarter == 0:
                build(source)
            spread[quarter] += product(source, quarter)

    def finish(q, running):
        mats = []
        for z in range(zq):
            flat = spread[q, z * BW : (z + 1) * BW, :].astype(BF16)
            mats.append(jnp.concatenate([flat[:, m * breadth : (m + 1) * breadth] for m in range(across)], axis=0))
        inscatter = jnp.dot(table_y[...], jnp.concatenate(mats, axis=1), preferred_element_type=F32)
        for z in range(zq):
            running = running + weight[q * zq + z] * inscatter[:, z * breadth : (z + 1) * breadth]
        return running

    def gather_early():
        early_all.wait_recv()
        early_all.wait_send()

        zero = jnp.zeros((band, breadth), F32)
        depth_sum, glow_sum, lit_sum = zero, zero, zero
        for k in range(depth_count):
            held = early_in[k].astype(F32)
            ahead = jnp.exp(-depth_sum)
            before[k] = ahead
            glow_sum = glow_sum + ahead * held[0:band]
            lit_sum = lit_sum + held[band : 2 * band]
            depth_sum = depth_sum + held[2 * band : 3 * band] + held[3 * band : 4 * band]
        passed = jnp.exp(-depth_sum)
        base[0] = glow_sum
        base[1] = lit_sum * passed
        base[2] = 1.0 - passed

    def settle(n):
        for sign in (-1, 1):
            send(n, sign).wait_send()
            hand_over(n, sign, True).wait_send()

    for n in range(steps):
        for sign in (-1, 1):
            received(n, sign).wait_recv()
            for m in onward(n, sign):
                send(m, sign).start()
        for sign in (-1, 1):
            hand_over(n, sign, True).start()
        if n >= BEHIND:
            collect(n - BEHIND)
        if n >= 2:
            settle(n - 2)
        if n == 2:
            for q in range(QUARTERS):
                own_part(q, tile).wait_send()
        pass_word(n + 1)
        if n + 1 == max(len(rounds), 1):
            for a, b in far_first:
                leaving(early_part, a, b).start()
        if n == steps - 4:
            gather_early()

    for n in range(steps - BEHIND, steps - 1):
        collect(n)
    running = finish(2, finish(0, jnp.zeros((height, breadth), F32)))
    collect(steps - 1)
    running = finish(3, finish(1, running))
    for d in range(depth_count):
        late_out[d] = running[d * band : (d + 1) * band, :]

    for a, b in far_first:
        leaving(late_part, a, b).start()

    late_in[depth] = late_out[depth]

    for n in range(steps - 2, steps):
        settle(n)
    late_all.wait_recv()
    scattered = jnp.sum(before[...] * late_in[...], axis=0)
    loads[2].wait()
    loads[3].wait()
    lit = base[1] + scattered
    for c in range(3):
        out_ref[c] = emit[c] * base[0] + albedo[c] * lit
    out_ref[3] = base[2]

    late_all.wait_send()


def shards(density, heat, emit_color, albedo, hot_order, hot_count):
    depth_count = lax.axis_size("depth")
    tile_count = lax.axis_size("tile")
    slices, height, breadth = density.shape
    chips = tile_count // 2
    steps = 2 * (chips - 1)
    rows = slices // QUARTERS * BW
    band = height // depth_count
    across = height // BW
    dma = pltpu.SemaphoreType.DMA
    anywhere = pl.BlockSpec(memory_space=pl.ANY)
    image = pl.pallas_call(
        functools.partial(render, depth_count, tile_count),
        out_shape=jax.ShapeDtypeStruct((4, band, breadth), F32),
        in_specs=[anywhere] * 6,
        out_specs=pl.BlockSpec(memory_space=pltpu.VMEM),
        scratch_shapes=[
            pltpu.SMEM((3,), F32), pltpu.SMEM((3,), F32), pltpu.SMEM((1, 16), jnp.int32), pltpu.SMEM((1,), jnp.int32),
            pltpu.VMEM((slices, height, breadth), BF16),
            pltpu.VMEM((slices, height, breadth), BF16),
            pltpu.VMEM((slices, height, breadth), F32),
            pltpu.VMEM((tile_count, HEAD + slices * BW, breadth), BF16),
            pltpu.VMEM((QUARTERS, rows, across * breadth), F32),
            pltpu.VMEM((chips, 2 * breadth, across * breadth), BF16),
            pltpu.VMEM((height, breadth), F32),
            pltpu.VMEM((height, breadth), BF16),
            pltpu.VMEM((4, height, breadth), F32),
            pltpu.VMEM((depth_count, 4 * band, breadth), BF16),
            pltpu.VMEM((depth_count, 4 * band, breadth), BF16),
            pltpu.VMEM((depth_count, band, breadth), F32),
            pltpu.VMEM((depth_count, band, breadth), F32),
            pltpu.VMEM((depth_count, band, breadth), F32),
            pltpu.VMEM((3, band, breadth), F32),
            dma((4,)), dma((QUARTERS,)), dma((QUARTERS,)),
            dma((QUARTERS,)), dma((QUARTERS,)),
            dma((steps,)), dma((steps,)), dma((steps,)), dma((steps,)),
            dma((steps,)), dma((steps,)), dma((steps,)), dma((steps,)),
            dma, dma, dma, dma,
            pltpu.SemaphoreType.REGULAR((8,)),
        ],
        compiler_params=pltpu.CompilerParams(
            collective_id=0, has_side_effects=True, vmem_limit_bytes=54400 * 1024
        ),
        cost_estimate=pl.CostEstimate(flops=3 * 10**9, bytes_accessed=2 * 1024 * 1024, transcendentals=10**6),
    )(density, heat, emit_color, albedo, hot_order, hot_count)
    return image.reshape(4, 1, band * breadth)


def solution(mesh):
    placed = (
        P("depth", None, "tile"),
        P("depth", None, "tile"),
        P(),
        P(),
        P("tile", None),
        P("tile"),
    )
    return jax.shard_map(
        shards, mesh=mesh, in_specs=placed, out_specs=P(None, "tile", "depth"), check_vma=False
    )
```

```python
import functools
import math

import jax
import jax.numpy as jnp
from jax import lax
from jax.experimental import pallas as pl
from jax.experimental.pallas import tpu as pltpu
from jax.sharding import PartitionSpec as P

BW = 32
HOT = 4
QUARTERS = 4
HEAD = 16
COLUMNS = 4
BEHIND = 3
F32 = jnp.float32
BF16 = jnp.bfloat16
MESH = pl.DeviceIdType.MESH


def iota(shape, axis):
    return lax.broadcasted_iota(jnp.int32, shape, axis)


def render(
    depth_count, tile_count,
    density_hbm, heat_hbm, emit_hbm, albedo_hbm, order_hbm, count_hbm,
    out_ref,
    emit, albedo, order, count, density, heat, weight, blocks, spread, tables, cosines, table_y, plane,
    early_out, early_in, late_out, late_in, before, base,
    scalar_sem, heat_sem, density_sem, own_send, own_recv, right_send, right_recv, left_send, left_recv,
    pair_right_send, pair_right_recv, pair_left_send, pair_left_recv,
    early_send, early_recv, late_send, late_recv, word,
):
    slices, height, breadth = density.shape
    chips = tile_count // 2
    steps = 2 * (chips - 1)
    zq = slices // QUARTERS
    rows = zq * BW
    band = height // depth_count
    depth = lax.axis_index("depth")
    tile = lax.axis_index("tile")
    chip = lax.div(tile, 2)
    core = tile - 2 * chip
    sibling = 2 * chip + 1 - core

    def turned(index, count):
        return jnp.where(index >= count, index - count, index)

    ring = [turned(chip + k, chips) for k in range(chips)]
    columns = min(COLUMNS, depth_count)
    planes = depth_count // columns
    z_here = lax.div(depth, columns)
    x_here = depth - z_here * columns
    z_ring = [turned(z_here + k, planes) for k in range(planes)]
    x_ring = [turned(x_here + k, columns) for k in range(columns)]

    def beside(size):
        return [1, size - 1] if size > 2 else [1] * (size - 1)

    x_beside = [(z_here * columns + x_ring[k], tile) for k in beside(columns)]
    z_beside = [(z_ring[k] * columns + x_here, tile) for k in beside(planes)]
    far_first = sorted(
        [(a, b) for a in range(planes) for b in range(columns) if a + b],
        key=lambda e: -min(e[0], planes - e[0]) - min(e[1], columns - e[1]),
    )

    def partner(a, b):
        return z_ring[a] * columns + x_ring[b]

    def at_tile(index):
        return (depth, index)

    def remote(src, dst, send, recv, device):
        return pltpu.make_async_remote_copy(
            src_ref=src, dst_ref=dst, send_sem=send, recv_sem=recv, device_id=device, device_id_type=MESH
        )

    head_part, tail_part = pl.ds(0, zq), pl.ds(zq, slices - zq)
    heat_loads = [
        pltpu.make_async_copy(heat_hbm.at[part], heat.at[part], heat_sem.at[i])
        for i, part in enumerate((head_part, tail_part))
    ]
    density_load = pltpu.make_async_copy(density_hbm, density, density_sem)
    scalars = [(order_hbm, order), (count_hbm, count), (emit_hbm, emit), (albedo_hbm, albedo)]
    loads = [pltpu.make_async_copy(src, dst, scalar_sem.at[i]) for i, (src, dst) in enumerate(scalars)]
    heat_loads[0].start()
    loads[0].start()
    loads[1].start()

    barrier = pltpu.get_barrier_semaphore()

    greeted = [(depth, 2 * ring[1] + core), (depth, 2 * ring[-1] + core), (depth, sibling)] + x_beside + z_beside
    for device in greeted:
        pl.semaphore_signal(barrier, inc=1, device_id=device, device_id_type=MESH)

    heat_loads[1].start()

    rounds = [x_beside] * (columns // 2 - 1) + [z_beside] * (planes // 2)

    def pass_word(r):
        if 0 < r <= len(rounds):
            pl.semaphore_wait(word.at[r - 1], len(rounds[r - 1]))
        if r < len(rounds):
            for device in rounds[r]:
                pl.semaphore_signal(word.at[r], inc=1, device_id=device, device_id_type=MESH)

    across = height // BW
    lane = iota((height, breadth), 1)
    row = iota((height, breadth), 0)
    lane_h = iota((HEAD, breadth), 1)
    row_h = iota((HEAD, breadth), 0)
    lead = iota((across * breadth, breadth), 0) - iota((across * breadth, breadth), 1) % BW
    slot_of = iota((across * breadth, breadth), 1) // BW
    place = jnp.zeros((across * breadth, breadth), jnp.int32)
    info = jnp.zeros((HEAD, breadth), jnp.int32)
    loads[0].wait()
    loads[1].wait()
    for s in range(HOT):
        brick = order[0, s]
        x0 = lax.rem(brick, across) * BW
        y0 = lax.div(brick, across) * BW
        dead = 1 - jnp.minimum(jnp.maximum(count[0] - s, 0), 1)
        first = lax.div(brick, across) * breadth + x0 + dead * (2 * across * breadth)
        place = jnp.where(slot_of == s, first, place)
        value = jnp.where(row_h == 0, y0, x0 + lane_h % BW)
        info = jnp.where(lane_h // BW == s, value, info)
    pick = jnp.where(lead == place, 1.0, 0.0).astype(BF16)
    blocks[tile, 0:HEAD, :] = info.astype(F32).astype(BF16)

    def pack(q):
        if q < 2:
            heat_loads[q].wait()
        pieces = [
            heat[q * zq : (q + 1) * zq, m * BW : (m + 1) * BW, :].reshape(rows, breadth) for m in range(across)
        ]
        packed = jnp.dot(jnp.concatenate(pieces, axis=1), pick, preferred_element_type=F32)
        blocks[tile, HEAD + q * rows : HEAD + (q + 1) * rows, :] = packed.astype(BF16)

    pack(0)
    pl.semaphore_wait(barrier, len(greeted))

    half = chips // 2
    order_of = {-1: [0, 1, 2, 3] * (half - 1) + [0, 1], 1: [0, 2, 3, 1] * (half - 1) + [2, 3]}

    def lines(q):
        return pl.ds(0, HEAD + rows) if q == 0 else pl.ds(HEAD + q * rows, rows)

    def block(group, q):
        return blocks.at[group, lines(q)]

    def ring_part(n, sign, source, device):
        sends, recvs = (right_send, right_recv) if sign < 0 else (left_send, left_recv)
        ref = block(2 * source + core, order_of[sign][n])
        return remote(ref, ref, sends.at[n], recvs.at[n], at_tile(device))

    def send(n, sign):
        return ring_part(n, sign, ring[sign * (n // QUARTERS)], 2 * ring[-sign] + core)

    def arrival(n, sign):
        return ring[sign * (n // QUARTERS + 1)], order_of[sign][n]

    def received(n, sign):
        return ring_part(n, sign, arrival(n, sign)[0], sibling)

    def onward(n, sign):
        later = [m for m in range(n + 1, steps) if m // QUARTERS == n // QUARTERS + 1]
        return [m for m in later if order_of[sign][m] == order_of[sign][n]]

    def hand_over(n, sign, mine):
        source, quarter = arrival(n, sign)
        sends, recvs = (pair_right_send, pair_right_recv) if sign < 0 else (pair_left_send, pair_left_recv)
        ref = block(2 * source + (core if mine else 1 - core), quarter)
        return remote(ref, ref, sends.at[n], recvs.at[n], at_tile(sibling))

    def own_part(q, group):
        ref = block(group, q)
        return remote(ref, ref, own_send.at[q], own_recv.at[q], at_tile(sibling))

    def early_part(target, source):
        return remote(early_out.at[target], early_in.at[source], early_send, early_recv, (target, tile))

    def late_part(target, source):
        return remote(late_out.at[target], late_in.at[source], late_send, late_recv, (target, tile))

    def leaving(part, a, b):
        return part(partner(a, b), depth)

    def everyone(out, into, send_sem, recv_sem):
        others = pl.ds(0, depth_count - 1)
        return remote(out.at[others], into.at[others], send_sem, recv_sem, (depth, sibling))

    early_all = everyone(early_out, early_in, early_send, early_recv)
    late_all = everyone(late_out, late_in, late_send, late_recv)

    for q in range(QUARTERS):
        if q > 0:
            pack(q)
        for sign in (-1, 1):
            for n in range(QUARTERS):
                if max(order_of[sign][: n + 1]) == q and (order_of[sign][n] == q or n == QUARTERS - 1):
                    send(n, sign).start()
        own_part(q, tile).start()
    pass_word(0)
    density_load.start()
    loads[2].start()
    loads[3].start()

    offset = iota((BW, breadth), 0) - iota((BW, breadth), 1)
    turn = (offset * offset) % (2 * BW)
    chirp = jnp.cos(turn.astype(F32) * (math.pi / BW) + math.pi / 8.0)
    for s in range(height // BW):
        cosines[pl.ds(s * BW, BW), :] = chirp
    ratio_y = (row - lane).astype(F32) / (height / 4.0)
    table_y[...] = (cosines[...] / (1.0 + ratio_y * ratio_y)).astype(BF16)

    density_load.wait()
    unit = 1.5 / (slices * depth_count)
    strip = 32

    @pl.loop(0, height // strip)
    def _(b):
        here = pl.ds(pl.multiple_of(b * strip, strip), strip)

        def slice_step(z, carry):
            total, trans, glow_sum, lit_sum = carry
            optical = density[z, here, :].astype(F32) * unit
            total = total + optical
            after = jnp.exp(-total)
            own = trans - after
            weight[z, here, :] = own
            glow_sum = glow_sum + own * heat[z, here, :].astype(F32)
            lit_sum = lit_sum + (jnp.exp(optical) - 1.0)
            return total, after, glow_sum, lit_sum

        zero = jnp.zeros((strip, breadth), F32)
        total, _, glow_sum, lit_sum = lax.fori_loop(
            0, slices, slice_step, (zero, jnp.ones_like(zero), zero, zero), unroll=4
        )
        plane[0, here, :] = glow_sum
        plane[1, here, :] = lit_sum
        high = total.astype(BF16).astype(F32)
        plane[2, here, :] = high
        plane[3, here, :] = total - high

    for d in range(depth_count):
        rows_d = [plane[p, d * band : (d + 1) * band, :] for p in range(4)]
        early_out[d] = jnp.concatenate(rows_d, axis=0).astype(BF16)

    early_in[depth] = early_out[depth]

    scale = 64.0 / (HOT * tile_count * BW)

    def build(source):
        for c in range(2):
            info_c = blocks[2 * source + c, 0:HEAD, :].astype(F32).T
            shift = ((tile - 2 * source - c) * breadth).astype(F32)
            ratio = (lane.astype(F32) + shift - info_c[:, 1:2]) / (tile_count * height / 2.0)
            value = scale * (cosines[...] / (1.0 + ratio * ratio))
            for m in range(across):
                held = jnp.where(info_c[:, 0:1] == float(m * BW), value, 0.0)
                tables[source, c * breadth : (c + 1) * breadth, m * breadth : (m + 1) * breadth] = held.astype(BF16)

    def product(source, q):
        part = slice(HEAD + q * rows, HEAD + (q + 1) * rows)
        left = jnp.concatenate([blocks[2 * source, part, :], blocks[2 * source + 1, part, :]], axis=1)
        return jnp.dot(left, tables[source], preferred_element_type=F32)

    own_part(0, sibling).wait_recv()
    build(chip)
    spread[0] = product(chip, 0)
    for q in range(1, QUARTERS):
        own_part(q, sibling).wait_recv()
        spread[q] = product(chip, q)

    def collect(n):
        for sign in (-1, 1):
            hand_over(n, sign, False).wait_recv()
        for sign in (-1, 1):
            source, quarter = arrival(n, sign)
            if quarter == 0:
                build(source)
            spread[quarter] += product(source, quarter)

    def finish(q, running):
        mats = []
        for z in range(zq):
            flat = spread[q, z * BW : (z + 1) * BW, :].astype(BF16)
            mats.append(jnp.concatenate([flat[:, m * breadth : (m + 1) * breadth] for m in range(across)], axis=0))
        inscatter = jnp.dot(table_y[...], jnp.concatenate(mats, axis=1), preferred_element_type=F32)
        for z in range(zq):
            running = running + weight[q * zq + z] * inscatter[:, z * breadth : (z + 1) * breadth]
        return running

    def gather_early():
        early_all.wait_recv()
        early_all.wait_send()

        zero = jnp.zeros((band, breadth), F32)
        depth_sum, glow_sum, lit_sum = zero, zero, zero
        for k in range(depth_count):
            held = early_in[k].astype(F32)
            ahead = jnp.exp(-depth_sum)
            before[k] = ahead
            glow_sum = glow_sum + ahead * held[0:band]
            lit_sum = lit_sum + held[band : 2 * band]
            depth_sum = depth_sum + held[2 * band : 3 * band] + held[3 * band : 4 * band]
        passed = jnp.exp(-depth_sum)
        base[0] = glow_sum
        base[1] = lit_sum * passed
        base[2] = 1.0 - passed

    def settle(n):
        for sign in (-1, 1):
            send(n, sign).wait_send()
            hand_over(n, sign, True).wait_send()

    for n in range(steps):
        for sign in (-1, 1):
            received(n, sign).wait_recv()
            for m in onward(n, sign):
                send(m, sign).start()
        for sign in (-1, 1):
            hand_over(n, sign, True).start()
        if n >= BEHIND:
            collect(n - BEHIND)
        if n >= 2:
            settle(n - 2)
        if n == 2:
            for q in range(QUARTERS):
                own_part(q, tile).wait_send()
        pass_word(n + 1)
        if n + 1 == max(len(rounds), 1):
            for a, b in far_first:
                leaving(early_part, a, b).start()
        if n == steps - 4:
            gather_early()

    for n in range(steps - BEHIND, steps - 1):
        collect(n)
    running = finish(2, finish(0, jnp.zeros((height, breadth), F32)))
    collect(steps - 1)
    running = finish(3, finish(1, running))
    for d in range(depth_count):
        late_out[d] = running[d * band : (d + 1) * band, :]
    for d in range(depth_count):

        @pl.when(depth != d)
        def _():
            late_part(d, depth).start()

    late_in[depth] = late_out[depth]

    for n in range(steps - 2, steps):
        settle(n)
    late_all.wait_recv()
    scattered = jnp.sum(before[...] * late_in[...], axis=0)
    loads[2].wait()
    loads[3].wait()
    lit = base[1] + scattered
    for c in range(3):
        out_ref[c] = emit[c] * base[0] + albedo[c] * lit
    out_ref[3] = base[2]

    late_all.wait_send()


def shards(density, heat, emit_color, albedo, hot_order, hot_count):
    depth_count = lax.axis_size("depth")
    tile_count = lax.axis_size("tile")
    slices, height, breadth = density.shape
    chips = tile_count // 2
    steps = 2 * (chips - 1)
    rows = slices // QUARTERS * BW
    band = height // depth_count
    across = height // BW
    dma = pltpu.SemaphoreType.DMA
    anywhere = pl.BlockSpec(memory_space=pl.ANY)
    image = pl.pallas_call(
        functools.partial(render, depth_count, tile_count),
        out_shape=jax.ShapeDtypeStruct((4, band, breadth), F32),
        in_specs=[anywhere] * 6,
        out_specs=pl.BlockSpec(memory_space=pltpu.VMEM),
        scratch_shapes=[
            pltpu.SMEM((3,), F32), pltpu.SMEM((3,), F32), pltpu.SMEM((1, 16), jnp.int32), pltpu.SMEM((1,), jnp.int32),
            pltpu.VMEM((slices, height, breadth), BF16),
            pltpu.VMEM((slices, height, breadth), BF16),
            pltpu.VMEM((slices, height, breadth), F32),
            pltpu.VMEM((tile_count, HEAD + slices * BW, breadth), BF16),
            pltpu.VMEM((QUARTERS, rows, across * breadth), F32),
            pltpu.VMEM((chips, 2 * breadth, across * breadth), BF16),
            pltpu.VMEM((height, breadth), F32),
            pltpu.VMEM((height, breadth), BF16),
            pltpu.VMEM((4, height, breadth), F32),
            pltpu.VMEM((depth_count, 4 * band, breadth), BF16),
            pltpu.VMEM((depth_count, 4 * band, breadth), BF16),
            pltpu.VMEM((depth_count, band, breadth), F32),
            pltpu.VMEM((depth_count, band, breadth), F32),
            pltpu.VMEM((depth_count, band, breadth), F32),
            pltpu.VMEM((3, band, breadth), F32),
            dma((4,)), dma((2,)), dma,
            dma((QUARTERS,)), dma((QUARTERS,)),
            dma((steps,)), dma((steps,)), dma((steps,)), dma((steps,)),
            dma((steps,)), dma((steps,)), dma((steps,)), dma((steps,)),
            dma, dma, dma, dma,
            pltpu.SemaphoreType.REGULAR((8,)),
        ],
        compiler_params=pltpu.CompilerParams(
            collective_id=0, has_side_effects=True, vmem_limit_bytes=54400 * 1024
        ),
        cost_estimate=pl.CostEstimate(flops=3 * 10**9, bytes_accessed=2 * 1024 * 1024, transcendentals=10**6),
    )(density, heat, emit_color, albedo, hot_order, hot_count)
    return image.reshape(4, 1, band * breadth)


def solution(mesh):
    placed = (
        P("depth", None, "tile"),
        P("depth", None, "tile"),
        P(),
        P(),
        P("tile", None),
        P("tile"),
    )
    return jax.shard_map(
        shards, mesh=mesh, in_specs=placed, out_specs=P(None, "tile", "depth"), check_vma=False
    )
```

```python
import functools
import math

import jax
import jax.numpy as jnp
from jax import lax
from jax.experimental import pallas as pl
from jax.experimental.pallas import tpu as pltpu
from jax.sharding import PartitionSpec as P

BW = 32
HOT = 4
QUARTERS = 4
HEAD = 16
COLUMNS = 4
BEHIND = 3
F32 = jnp.float32
BF16 = jnp.bfloat16
MESH = pl.DeviceIdType.MESH


def iota(shape, axis):
    return lax.broadcasted_iota(jnp.int32, shape, axis)


def render(
    depth_count, tile_count,
    density_hbm, heat_hbm, emit_hbm, albedo_hbm, order_hbm, count_hbm,
    out_ref,
    emit, albedo, order, count, density, heat, weight, blocks, spread, tables, cosines, table_y, plane,
    early_out, early_in, late_out, late_in, before, base,
    scalar_sem, heat_sem, density_sem, own_send, own_recv, right_send, right_recv, left_send, left_recv,
    pair_right_send, pair_right_recv, pair_left_send, pair_left_recv,
    early_send, early_recv, late_send, late_recv, word,
):
    slices, height, breadth = density.shape
    chips = tile_count // 2
    steps = 2 * (chips - 1)
    zq = slices // QUARTERS
    rows = zq * BW
    band = height // depth_count
    depth = lax.axis_index("depth")
    tile = lax.axis_index("tile")
    chip = lax.div(tile, 2)
    core = tile - 2 * chip
    sibling = 2 * chip + 1 - core

    def turned(index, count):
        return jnp.where(index >= count, index - count, index)

    ring = [turned(chip + k, chips) for k in range(chips)]
    columns = min(COLUMNS, depth_count)
    planes = depth_count // columns
    z_here = lax.div(depth, columns)
    x_here = depth - z_here * columns
    z_ring = [turned(z_here + k, planes) for k in range(planes)]
    x_ring = [turned(x_here + k, columns) for k in range(columns)]

    def beside(size):
        return [1, size - 1] if size > 2 else [1] * (size - 1)

    x_beside = [(z_here * columns + x_ring[k], tile) for k in beside(columns)]
    z_beside = [(z_ring[k] * columns + x_here, tile) for k in beside(planes)]
    far_first = sorted(
        [(a, b) for a in range(planes) for b in range(columns) if a + b],
        key=lambda e: -min(e[0], planes - e[0]) - min(e[1], columns - e[1]),
    )

    def partner(a, b):
        return z_ring[a] * columns + x_ring[b]

    def at_tile(index):
        return (depth, index)

    def remote(src, dst, send, recv, device):
        return pltpu.make_async_remote_copy(
            src_ref=src, dst_ref=dst, send_sem=send, recv_sem=recv, device_id=device, device_id_type=MESH
        )

    head_part, tail_part = pl.ds(0, zq), pl.ds(zq, slices - zq)
    heat_loads = [
        pltpu.make_async_copy(heat_hbm.at[part], heat.at[part], heat_sem.at[i])
        for i, part in enumerate((head_part, tail_part))
    ]
    density_load = pltpu.make_async_copy(density_hbm, density, density_sem)
    scalars = [(order_hbm, order), (count_hbm, count), (emit_hbm, emit), (albedo_hbm, albedo)]
    loads = [pltpu.make_async_copy(src, dst, scalar_sem.at[i]) for i, (src, dst) in enumerate(scalars)]
    heat_loads[0].start()
    loads[0].start()
    loads[1].start()

    barrier = pltpu.get_barrier_semaphore()

    greeted = [(depth, 2 * ring[1] + core), (depth, 2 * ring[-1] + core), (depth, sibling)] + x_beside + z_beside
    for device in greeted:
        pl.semaphore_signal(barrier, inc=1, device_id=device, device_id_type=MESH)

    heat_loads[1].start()

    rounds = [x_beside] * (columns // 2 - 1) + [z_beside] * (planes // 2)

    def pass_word(r):
        if 0 < r <= len(rounds):
            pl.semaphore_wait(word.at[r - 1], len(rounds[r - 1]))
        if r < len(rounds):
            for device in rounds[r]:
                pl.semaphore_signal(word.at[r], inc=1, device_id=device, device_id_type=MESH)

    across = height // BW
    lane = iota((height, breadth), 1)
    row = iota((height, breadth), 0)
    lane_h = iota((HEAD, breadth), 1)
    row_h = iota((HEAD, breadth), 0)
    lead = iota((across * breadth, breadth), 0) - iota((across * breadth, breadth), 1) % BW
    slot_of = iota((across * breadth, breadth), 1) // BW
    place = jnp.zeros((across * breadth, breadth), jnp.int32)
    info = jnp.zeros((HEAD, breadth), jnp.int32)
    loads[0].wait()
    loads[1].wait()
    for s in range(HOT):
        brick = order[0, s]
        x0 = lax.rem(brick, across) * BW
        y0 = lax.div(brick, across) * BW
        dead = 1 - jnp.minimum(jnp.maximum(count[0] - s, 0), 1)
        first = lax.div(brick, across) * breadth + x0 + dead * (2 * across * breadth)
        place = jnp.where(slot_of == s, first, place)
        value = jnp.where(row_h == 0, y0, x0 + lane_h % BW)
        info = jnp.where(lane_h // BW == s, value, info)
    pick = jnp.where(lead == place, 1.0, 0.0).astype(BF16)
    blocks[tile, 0:HEAD, :] = info.astype(F32).astype(BF16)

    def pack(q):
        if q < 2:
            heat_loads[q].wait()
        pieces = [
            heat[q * zq : (q + 1) * zq, m * BW : (m + 1) * BW, :].reshape(rows, breadth) for m in range(across)
        ]
        packed = jnp.dot(jnp.concatenate(pieces, axis=1), pick, preferred_element_type=F32)
        blocks[tile, HEAD + q * rows : HEAD + (q + 1) * rows, :] = packed.astype(BF16)

    pack(0)
    pl.semaphore_wait(barrier, len(greeted))

    half = chips // 2
    order_of = {-1: [0, 1, 2, 3] * (half - 1) + [0, 1], 1: [0, 2, 3, 1] * (half - 1) + [2, 3]}

    def lines(q):
        return pl.ds(0, HEAD + rows) if q == 0 else pl.ds(HEAD + q * rows, rows)

    def block(group, q):
        return blocks.at[group, lines(q)]

    def ring_part(n, sign, source, device):
        sends, recvs = (right_send, right_recv) if sign < 0 else (left_send, left_recv)
        ref = block(2 * source + core, order_of[sign][n])
        return remote(ref, ref, sends.at[n], recvs.at[n], at_tile(device))

    def send(n, sign):
        return ring_part(n, sign, ring[sign * (n // QUARTERS)], 2 * ring[-sign] + core)

    def arrival(n, sign):
        return ring[sign * (n // QUARTERS + 1)], order_of[sign][n]

    def received(n, sign):
        return ring_part(n, sign, arrival(n, sign)[0], sibling)

    def onward(n, sign):
        later = [m for m in range(n + 1, steps) if m // QUARTERS == n // QUARTERS + 1]
        return [m for m in later if order_of[sign][m] == order_of[sign][n]]

    def hand_over(n, sign, mine):
        source, quarter = arrival(n, sign)
        sends, recvs = (pair_right_send, pair_right_recv) if sign < 0 else (pair_left_send, pair_left_recv)
        ref = block(2 * source + (core if mine else 1 - core), quarter)
        return remote(ref, ref, sends.at[n], recvs.at[n], at_tile(sibling))

    def own_part(q, group):
        ref = block(group, q)
        return remote(ref, ref, own_send.at[q], own_recv.at[q], at_tile(sibling))

    def early_part(target, source):
        return remote(early_out.at[target], early_in.at[source], early_send, early_recv, (target, tile))

    def late_part(target, source):
        return remote(late_out.at[target], late_in.at[source], late_send, late_recv, (target, tile))

    def leaving(part, a, b):
        return part(partner(a, b), depth)

    def everyone(out, into, send_sem, recv_sem):
        others = pl.ds(0, depth_count - 1)
        return remote(out.at[others], into.at[others], send_sem, recv_sem, (depth, sibling))

    early_all = everyone(early_out, early_in, early_send, early_recv)
    late_all = everyone(late_out, late_in, late_send, late_recv)

    for q in range(QUARTERS):
        if q > 0:
            pack(q)
        for sign in (-1, 1):
            for n in range(QUARTERS):
                if max(order_of[sign][: n + 1]) == q and (order_of[sign][n] == q or n == QUARTERS - 1):
                    send(n, sign).start()
        own_part(q, tile).start()
    pass_word(0)
    density_load.start()
    loads[2].start()
    loads[3].start()

    offset = iota((BW, breadth), 0) - iota((BW, breadth), 1)
    turn = (offset * offset) % (2 * BW)
    chirp = jnp.cos(turn.astype(F32) * (math.pi / BW) + math.pi / 8.0)
    for s in range(height // BW):
        cosines[pl.ds(s * BW, BW), :] = chirp
    ratio_y = (row - lane).astype(F32) / (height / 4.0)
    table_y[...] = (cosines[...] / (1.0 + ratio_y * ratio_y)).astype(BF16)

    density_load.wait()
    unit = 1.5 / (slices * depth_count)
    strip = 32

    @pl.loop(0, height // strip)
    def _(b):
        here = pl.ds(pl.multiple_of(b * strip, strip), strip)

        def slice_step(z, carry):
            total, trans, glow_sum, lit_sum = carry
            optical = density[z, here, :].astype(F32) * unit
            total = total + optical
            after = jnp.exp(-total)
            own = trans - after
            weight[z, here, :] = own
            glow_sum = glow_sum + own * heat[z, here, :].astype(F32)
            lit_sum = lit_sum + (jnp.exp(optical) - 1.0)
            return total, after, glow_sum, lit_sum

        zero = jnp.zeros((strip, breadth), F32)
        total, _, glow_sum, lit_sum = lax.fori_loop(
            0, slices, slice_step, (zero, jnp.ones_like(zero), zero, zero), unroll=4
        )
        plane[0, here, :] = glow_sum
        plane[1, here, :] = lit_sum
        high = total.astype(BF16).astype(F32)
        plane[2, here, :] = high
        plane[3, here, :] = total - high

    for d in range(depth_count):
        rows_d = [plane[p, d * band : (d + 1) * band, :] for p in range(4)]
        early_out[d] = jnp.concatenate(rows_d, axis=0).astype(BF16)

    early_in[depth] = early_out[depth]

    scale = 64.0 / (HOT * tile_count * BW)

    def build(source):
        for c in range(2):
            info_c = blocks[2 * source + c, 0:HEAD, :].astype(F32).T
            shift = ((tile - 2 * source - c) * breadth).astype(F32)
            ratio = (lane.astype(F32) + shift - info_c[:, 1:2]) / (tile_count * height / 2.0)
            value = scale * (cosines[...] / (1.0 + ratio * ratio))
            for m in range(across):
                held = jnp.where(info_c[:, 0:1] == float(m * BW), value, 0.0)
                tables[source, c * breadth : (c + 1) * breadth, m * breadth : (m + 1) * breadth] = held.astype(BF16)

    def product(source, q):
        part = slice(HEAD + q * rows, HEAD + (q + 1) * rows)
        left = jnp.concatenate([blocks[2 * source, part, :], blocks[2 * source + 1, part, :]], axis=1)
        return jnp.dot(left, tables[source], preferred_element_type=F32)

    own_part(0, sibling).wait_recv()
    build(chip)
    spread[0] = product(chip, 0)
    for q in range(1, QUARTERS):
        own_part(q, sibling).wait_recv()
        spread[q] = product(chip, q)

    def collect(n):
        for sign in (-1, 1):
            hand_over(n, sign, False).wait_recv()
        for sign in (-1, 1):
            source, quarter = arrival(n, sign)
            if quarter == 0:
                build(source)
            spread[quarter] += product(source, quarter)

    def finish(quarters, running):
        mats, slabs = [], []
        for q in quarters:
            for z in range(zq):
                flat = spread[q, z * BW : (z + 1) * BW, :].astype(BF16)
                pieces = [flat[:, m * breadth : (m + 1) * breadth] for m in range(across)]
                mats.append(jnp.concatenate(pieces, axis=0))
                slabs.append(q * zq + z)
        inscatter = jnp.dot(table_y[...], jnp.concatenate(mats, axis=1), preferred_element_type=F32)
        for i, z in enumerate(slabs):
            running = running + weight[z] * inscatter[:, i * breadth : (i + 1) * breadth]
        return running

    def gather_early():
        early_all.wait_recv()
        early_all.wait_send()

        zero = jnp.zeros((band, breadth), F32)
        depth_sum, glow_sum, lit_sum = zero, zero, zero
        for k in range(depth_count):
            held = early_in[k].astype(F32)
            ahead = jnp.exp(-depth_sum)
            before[k] = ahead
            glow_sum = glow_sum + ahead * held[0:band]
            lit_sum = lit_sum + held[band : 2 * band]
            depth_sum = depth_sum + held[2 * band : 3 * band] + held[3 * band : 4 * band]
        passed = jnp.exp(-depth_sum)
        base[0] = glow_sum
        base[1] = lit_sum * passed
        base[2] = 1.0 - passed

    def settle(n):
        for sign in (-1, 1):
            send(n, sign).wait_send()
            hand_over(n, sign, True).wait_send()

    for n in range(steps):
        for sign in (-1, 1):
            received(n, sign).wait_recv()
            for m in onward(n, sign):
                send(m, sign).start()
        for sign in (-1, 1):
            hand_over(n, sign, True).start()
        if n >= BEHIND:
            collect(n - BEHIND)
        if n >= 2:
            settle(n - 2)
        if n == 2:
            for q in range(QUARTERS):
                own_part(q, tile).wait_send()
        pass_word(n + 1)
        if n + 1 == max(len(rounds), 1):
            for a, b in far_first:
                leaving(early_part, a, b).start()
        if n == steps - 4:
            gather_early()

    for n in range(steps - BEHIND, steps - 1):
        collect(n)
    running = finish((0, 2), jnp.zeros((height, breadth), F32))
    collect(steps - 1)
    running = finish((1, 3), running)
    for d in range(depth_count):
        late_out[d] = running[d * band : (d + 1) * band, :]
    for d in range(depth_count):

        @pl.when(depth != d)
        def _():
            late_part(d, depth).start()

    late_in[depth] = late_out[depth]

    for n in range(steps - 2, steps):
        settle(n)
    late_all.wait_recv()
    scattered = jnp.sum(before[...] * late_in[...], axis=0)
    loads[2].wait()
    loads[3].wait()
    lit = base[1] + scattered
    for c in range(3):
        out_ref[c] = emit[c] * base[0] + albedo[c] * lit
    out_ref[3] = base[2]

    late_all.wait_send()


def shards(density, heat, emit_color, albedo, hot_order, hot_count):
    depth_count = lax.axis_size("depth")
    tile_count = lax.axis_size("tile")
    slices, height, breadth = density.shape
    chips = tile_count // 2
    steps = 2 * (chips - 1)
    rows = slices // QUARTERS * BW
    band = height // depth_count
    across = height // BW
    dma = pltpu.SemaphoreType.DMA
    anywhere = pl.BlockSpec(memory_space=pl.ANY)
    image = pl.pallas_call(
        functools.partial(render, depth_count, tile_count),
        out_shape=jax.ShapeDtypeStruct((4, band, breadth), F32),
        in_specs=[anywhere] * 6,
        out_specs=pl.BlockSpec(memory_space=pltpu.VMEM),
        scratch_shapes=[
            pltpu.SMEM((3,), F32), pltpu.SMEM((3,), F32), pltpu.SMEM((1, 16), jnp.int32), pltpu.SMEM((1,), jnp.int32),
            pltpu.VMEM((slices, height, breadth), BF16),
            pltpu.VMEM((slices, height, breadth), BF16),
            pltpu.VMEM((slices, height, breadth), F32),
            pltpu.VMEM((tile_count, HEAD + slices * BW, breadth), BF16),
            pltpu.VMEM((QUARTERS, rows, across * breadth), F32),
            pltpu.VMEM((chips, 2 * breadth, across * breadth), BF16),
            pltpu.VMEM((height, breadth), F32),
            pltpu.VMEM((height, breadth), BF16),
            pltpu.VMEM((4, height, breadth), F32),
            pltpu.VMEM((depth_count, 4 * band, breadth), BF16),
            pltpu.VMEM((depth_count, 4 * band, breadth), BF16),
            pltpu.VMEM((depth_count, band, breadth), F32),
            pltpu.VMEM((depth_count, band, breadth), F32),
            pltpu.VMEM((depth_count, band, breadth), F32),
            pltpu.VMEM((3, band, breadth), F32),
            dma((4,)), dma((2,)), dma,
            dma((QUARTERS,)), dma((QUARTERS,)),
            dma((steps,)), dma((steps,)), dma((steps,)), dma((steps,)),
            dma((steps,)), dma((steps,)), dma((steps,)), dma((steps,)),
            dma, dma, dma, dma,
            pltpu.SemaphoreType.REGULAR((8,)),
        ],
        compiler_params=pltpu.CompilerParams(
            collective_id=0, has_side_effects=True, vmem_limit_bytes=54400 * 1024
        ),
        cost_estimate=pl.CostEstimate(flops=3 * 10**9, bytes_accessed=2 * 1024 * 1024, transcendentals=10**6),
    )(density, heat, emit_color, albedo, hot_order, hot_count)
    return image.reshape(4, 1, band * breadth)


def solution(mesh):
    placed = (
        P("depth", None, "tile"),
        P("depth", None, "tile"),
        P(),
        P(),
        P("tile", None),
        P("tile"),
    )
    return jax.shard_map(
        shards, mesh=mesh, in_specs=placed, out_specs=P(None, "tile", "depth"), check_vma=False
    )
```
